512 devices in a mesh: chan: 16 (over y_lo, x, core), slab: 32 (over y_hi, z).
Axes of the slice: x: 4, y: 4 (y_hi: 2, y_lo: 2; y = y_hi * 2 + y_lo), z: 16, core: 2. Of those that a mesh axis runs over, the one named last changes fastest.
Arguments:
- features: bfloat16 [128, 64, 8, 128], P('chan', 'slab'), may hold values from -6 to 6
- kernel: bfloat16 [27, 256, 128], P(None, 'chan'), may hold values from -0.109375 to 0.109375
- upstream: bfloat16 [256, 64, 8, 128], P('chan', 'slab'), may hold values from -6 to 6
Outputs:
- activated: bfloat16 [256, 64, 8, 128], P('chan', 'slab')
- input_grad: float32 [128, 64, 8, 128], P('chan', 'slab')
- kernel_grad: float32 [27, 256, 128], P(None, 'chan')
The draws below stay inside these ranges and needn't reach their ends.
All inputs are finite; a program needn't handle non-finite values.
Results may differ from the reference program's by a relative error of at most 0.0029.
Values may be sent and summed in bfloat16 or wider, within the bound.
A program may use at most 128 MiB of HBM per device.

```python
import jax
import jax.numpy as jnp
from jax import lax

C = 128
F = 256
TAPS = 27
NY = 8
NX = 128
NZ = 64


def steps_of(key, extent, pieces, smallest, largest):
    def one(dim, blocks):
        heights = jax.random.uniform(jax.random.fold_in(jax.random.fold_in(key, 6), dim), (blocks,), jnp.float32, smallest / len(pieces), largest / len(pieces))
        return jnp.repeat(jnp.exp(heights), extent[dim] // blocks).reshape((-1,) + (1,) * (len(extent) - dim - 1))

    gain = one(*pieces[0])
    for cut in pieces[1:]:
        gain = gain * one(*cut)
    return gain


def centred(key, extent, scale, most, cuts=(), kind=jnp.bfloat16):
    values = jax.random.normal(key, extent, jnp.float32) * scale
    if len(cuts) > 0:
        values = steps_of(key, extent, cuts, -0.22, 0.18) * values
    return jnp.clip(values, min=-most, max=most).astype(kind)


def setup_inputs(seed: int = 0) -> dict:
    key_list = jax.random.split(jax.random.key(seed), 4)
    return {
        "features": centred(key_list[0], (C, NZ, NY, NX), 1.0, 6.0, ((0, 16), (1, 32))),
        "kernel": centred(key_list[1], (TAPS, F, C), (TAPS * C) ** -0.5, 0.109375, ((1, 16),)),
        "upstream": centred(key_list[2], (F, NZ, NY, NX), 1.0, 6.0, ((0, 16), (1, 32))),
    }


def convolve(volume, weights):
    rhs = jnp.transpose(weights.reshape(3, 3, 3, weights.shape[1], weights.shape[2]), (3, 4, 0, 1, 2))
    result = lax.conv_general_dilated(volume[None], rhs, (1, 1, 1), ((1, 1), (1, 1), (1, 1)), dimension_numbers=('NCDHW', 'OIDHW', 'NCDHW'), precision=lax.Precision.HIGHEST)
    return result[0]

def reference(features, kernel, upstream):
    volume = features.astype(jnp.float32)
    weights = kernel.astype(jnp.float32)
    pre, pullback = jax.vjp(convolve, volume, weights)
    sigma = 1.0 / (1.0 + jnp.exp(-pre))
    activated = (pre * sigma).astype(jnp.bfloat16)
    delta = (upstream.astype(jnp.float32) * sigma * (1.0 + pre * (1.0 - sigma))).astype(jnp.bfloat16)
    input_grad, kernel_grad = pullback(delta.astype(jnp.float32))
    return (activated, input_grad, kernel_grad)
```

```python
import functools

import jax
import jax.numpy as jnp
from jax import lax
from jax.experimental import pallas as pl
from jax.experimental.pallas import tpu as pltpu
from jax.sharding import PartitionSpec as P

MESH = pl.DeviceIdType.MESH
F32 = jnp.float32
BF16 = jnp.bfloat16
CB = 8
FB = 16
NX = 128


def dot(a, b):
    return lax.dot_general(a, b, (((1,), (0,)), ((), ())), preferred_element_type=F32)


def dot_nt(a, b):
    return lax.dot_general(a, b, (((1,), (1,)), ((), ())), preferred_element_type=F32)


def shifted(v, lane):
    left = jnp.where(lane == NX - 1, 0.0, pltpu.roll(v, NX - 1, 1))
    right = jnp.where(lane == 0, 0.0, pltpu.roll(v, 1, 1))
    return left, right


def body(
    grid, ns, tp,
    feat_hbm, kern_hbm, up_hbm,
    act_ref, ig_ref, kg_ref,
    feat, kern, up, rows_f, rows_u, land, xc, tacc, w4, wt, d1, dh, d3, kgs, rsb, agb, kgown, igs, igr,
    in_sem, g_send, g_recv, f_send, h_send, h_recv, dh_send, dh_recv, rs_send, rs_recv, ag_send, ag_recv, ig_send, ig_recv,
):
    nyl, nxc = grid
    chips = nyl * nxc
    nchan = 2 * chips
    chans = nchan * CB
    owners = -(-27 // tp)
    me = lax.axis_index("chan")
    slab = lax.axis_index("slab")
    core = lax.rem(me, 2)
    chip = me // 2
    cx = lax.rem(chip, nxc)
    cy = chip // nxc
    sib = chip * 2 + (1 - core)

    loads = [
        pltpu.make_async_copy(feat_hbm, feat, in_sem.at[0]),
        pltpu.make_async_copy(kern_hbm, kern, in_sem.at[1]),
        pltpu.make_async_copy(up_hbm, up, in_sem.at[2]),
    ]
    for load in loads:
        load.start()

    barrier = pltpu.get_barrier_semaphore()

    def greet_chan(k, carry):
        pl.semaphore_signal(barrier, inc=1, device_id=(lax.rem(me + k, nchan), slab), device_id_type=MESH)
        return carry

    def greet_slab(k, carry):
        pl.semaphore_signal(barrier, inc=1, device_id=(me, lax.rem(slab + k, ns)), device_id_type=MESH)
        return carry

    lax.fori_loop(1, nchan, greet_chan, 0)
    lax.fori_loop(1, ns, greet_slab, 0)

    loads[0].wait()
    rows_f[...] = feat[...].astype(F32).reshape(CB * 16, NX)
    for z in range(2):
        for yp in range(4):
            pair = [rows_f[pl.ds(z * 8 + 2 * yp + k, CB, stride=16), :] for k in range(2)]
            land[me, 0, z * 4 + yp] = jnp.concatenate(pair, 0).astype(BF16)

    pl.semaphore_wait(barrier, nchan + ns - 2)

    up_halo = pltpu.make_async_remote_copy(
        src_ref=land.at[me, 0, pl.ds(4, 4)], dst_ref=land.at[me, 1, pl.ds(0, 4)],
        send_sem=h_send.at[0], recv_sem=h_recv.at[0], device_id=(me, slab + 1), device_id_type=MESH)
    down_halo = pltpu.make_async_remote_copy(
        src_ref=land.at[me, 0, pl.ds(0, 4)], dst_ref=land.at[me, 1, pl.ds(4, 4)],
        send_sem=h_send.at[1], recv_sem=h_recv.at[1], device_id=(me, slab - 1), device_id_type=MESH)

    @pl.when(slab < ns - 1)
    def _():
        up_halo.start()

    @pl.when(slab > 0)
    def _():
        down_halo.start()

    hops = [(j, k) for j in range(nyl) for k in range(nxc)][1:]

    def peer(j, k):
        return (lax.rem(cy + j, nyl) * nxc + lax.rem(cx + k, nxc)) * 2 + core

    def source(j, k):
        return (lax.rem(cy + nyl - j, nyl) * nxc + lax.rem(cx + nxc - k, nxc)) * 2 + core

    def gather_copy(part, holder, target, send_sem):
        return pltpu.make_async_remote_copy(
            src_ref=land.at[holder, part], dst_ref=land.at[holder, part],
            send_sem=send_sem, recv_sem=g_recv.at[part, holder], device_id=(target, slab), device_id_type=MESH)

    sent = []

    def send_own(part):
        for n, (j, k) in enumerate(hops):
            copy = gather_copy(part, me, peer(j, k), g_send.at[part, n])
            copy.start()
            sent.append(copy)
        copy = gather_copy(part, me, sib, g_send.at[part, chips - 1])
        copy.start()
        sent.append(copy)

    def forward(part):
        for n, (j, k) in enumerate(hops):
            holder = source(j, k)
            copy = gather_copy(part, holder, sib, f_send.at[part, n])
            copy.wait_recv()
            copy.start()
            sent.append(copy)

    def receive_rest(part):
        for q in range(chips):
            holder = lax.rem(chip + q, chips) * 2 + (1 - core)
            gather_copy(part, holder, sib, f_send.at[part, 0]).wait_recv()

    send_own(0)

    loads[1].wait()
    for a in range(3):
        taps = [kern[pl.ds(9 * a + 3 * b, 3)].reshape(3 * FB, chans) for b in range(3)]
        zero = jnp.zeros((3 * FB, chans), BF16)
        w4[a] = jnp.concatenate(
            [
                jnp.concatenate([taps[2], zero], 1),
                jnp.concatenate([taps[1], taps[2]], 1),
                jnp.concatenate([taps[0], taps[1]], 1),
                jnp.concatenate([zero, taps[0]], 1),
            ],
            0,
        )
    d3[...] = jnp.zeros(d3.shape, BF16)

    @pl.when(slab == 0)
    def _():
        land[me, 1, pl.ds(0, 4)] = jnp.zeros((4, 16, NX), BF16)

    @pl.when(slab == ns - 1)
    def _():
        land[me, 1, pl.ds(4, 4)] = jnp.zeros((4, 16, NX), BF16)

    @pl.when(slab > 0)
    def _():
        up_halo.wait_recv()

    @pl.when(slab < ns - 1)
    def _():
        down_halo.wait_recv()

    send_own(1)

    flipped = [kern[9 * a + 3 * b + e].astype(F32) for a in (2, 1, 0) for b in (2, 1, 0) for e in range(3)]
    flipped += [jnp.zeros((FB, chans), F32)] * 5
    for q in range(4):
        wt[:, pl.ds(q * 128, 128)] = jnp.transpose(jnp.concatenate(flipped[8 * q : 8 * q + 8], 0)).astype(BF16)

    loads[2].wait()
    rows_u[...] = up[...].astype(F32).reshape(FB * 16, NX)

    def unpack(part):
        for zi in range(2):
            z = (1, 2)[zi] if part == 0 else (0, 3)[zi]
            for yp in range(4):
                tiles = land[:, part, zi * 4 + yp].astype(F32)
                for k in range(2):
                    xc[z, 2 * yp + k] = tiles[:, CB * k : CB * k + CB].reshape(chans, NX).astype(BF16)

    def pair_rows(z, yp):
        return xc[z, pl.ds(2 * yp, 2)].reshape(2 * chans, NX)

    forward(0)
    receive_rest(0)
    unpack(0)
    for o in range(2):
        weights = jnp.concatenate([w4[1 - o], w4[2 - o]], 1)
        for q in range(2):
            cells = jnp.concatenate(
                [jnp.concatenate([pair_rows(z, 2 * q + k) for z in (1, 2)], 0) for k in range(2)], 1)
            tacc[o, q] = dot(weights, cells)

    forward(1)
    receive_rest(1)
    unpack(1)
    for o in range(2):
        for q in range(2):
            cells = jnp.concatenate([pair_rows(3 * o, 2 * q + k) for k in range(2)], 1)
            tacc[o, q] += dot(w4[2 * o], cells)

    lane = lax.broadcasted_iota(jnp.int32, (FB, NX), 1)

    def pair_sum(o, yp, yo):
        return tacc[o, yp // 2, pl.ds(yo * 3 * FB, 3 * FB), pl.ds((yp % 2) * NX, NX)]

    acts = []
    for o in range(2):
        for y in range(8):
            yp, r = y // 2, y % 2
            total = pair_sum(o, yp, 1 + r)
            if r == 0 and yp > 0:
                total = total + pair_sum(o, yp - 1, 3)
            if r == 1 and yp < 3:
                total = total + pair_sum(o, yp + 1, 0)
            from_left = shifted(total[0:FB], lane)[1]
            from_right = shifted(total[2 * FB : 3 * FB], lane)[0]
            pre = total[FB : 2 * FB] + from_left + from_right
            s = 1.0 / (1.0 + jnp.exp(-jnp.maximum(pre, -88.0)))
            upstream = rows_u[pl.ds(o * 8 + y, FB, stride=16), :]
            delta = (upstream * s * (1.0 + pre * (1.0 - s))).astype(BF16)
            rows_u[pl.ds(o * 8 + y, FB, stride=16), :] = pre * s
            d1[o, y] = delta
            left, right = shifted(delta.astype(F32), lane)
            d3[1 + o, 1 + y] = jnp.concatenate([left.astype(BF16), delta, right.astype(BF16)], 0)

    up_delta = pltpu.make_async_remote_copy(
        src_ref=d1.at[1], dst_ref=dh.at[0],
        send_sem=dh_send.at[0], recv_sem=dh_recv.at[0], device_id=(me, slab + 1), device_id_type=MESH)
    down_delta = pltpu.make_async_remote_copy(
        src_ref=d1.at[0], dst_ref=dh.at[1],
        send_sem=dh_send.at[1], recv_sem=dh_recv.at[1], device_id=(me, slab - 1), device_id_type=MESH)

    @pl.when(slab < ns - 1)
    def _():
        up_delta.start()

    @pl.when(slab > 0)
    def _():
        down_delta.start()

    for a in range(3):
        lhs = jnp.concatenate(
            [d3[1 + o, pl.ds(2 * yp, 4)].reshape(12 * FB, NX) for o in range(2) for yp in range(4)], 1)
        rhs = jnp.concatenate([pair_rows(o + a, yp) for o in range(2) for yp in range(4)], 1)
        g = dot_nt(lhs, rhs)
        for b in range(3):
            term = (
                g[(2 - b) * 3 * FB : (3 - b) * 3 * FB, :chans] + g[(3 - b) * 3 * FB : (4 - b) * 3 * FB, chans:]
            )
            kgs[pl.ds(9 * a + 3 * b, 3)] = term.reshape(3, FB, chans).astype(BF16)

    def term_copy(k):
        owner = lax.rem(slab + k, ns)
        return owner, pltpu.make_async_remote_copy(
            src_ref=kgs.at[pl.ds(lax.rem(owner, owners) * tp, tp)], dst_ref=rsb.at[k - 1],
            send_sem=rs_send, recv_sem=rs_recv, device_id=(me, owner), device_id_type=MESH)

    def send_term(k, carry):
        owner, copy = term_copy(k)

        @pl.when(owner < owners)
        def _():
            copy.start()

        return carry

    lax.fori_loop(1, ns, send_term, 0)

    act_ref[...] = rows_u[...].reshape(FB, 2, 8, NX).astype(BF16)

    def place_halo(plane, z):
        for y in range(8):
            delta = dh[plane, y]
            left, right = shifted(delta.astype(F32), lane)
            d3[z, 1 + y] = jnp.concatenate([left.astype(BF16), delta, right.astype(BF16)], 0)

    @pl.when(slab > 0)
    def _():
        up_delta.wait_recv()
        place_halo(0, 0)

    @pl.when(slab < ns - 1)
    def _():
        down_delta.wait_recv()
        place_halo(1, 3)

    blank = jnp.zeros((80, 2 * NX), BF16)
    for o in range(2):
        for yp in range(4):
            cells = jnp.concatenate(
                [
                    jnp.concatenate(
                        [d3[o + z, pl.ds(2 * yp + k, 3)].reshape(9 * FB, NX) for z in range(3)], 0)
                    for k in range(2)
                ],
                1,
            )
            grad = dot(wt[...], jnp.concatenate([cells, blank], 0)).reshape(nchan, CB, 2 * NX)
            igs[:, o * 4 + yp] = jnp.concatenate([grad[:, :, :NX], grad[:, :, NX:]], 1).astype(BF16)

    def grad_copy(k):
        target = lax.rem(me + k, nchan)
        return pltpu.make_async_remote_copy(
            src_ref=igs.at[target], dst_ref=igr.at[k - 1],
            send_sem=ig_send, recv_sem=ig_recv, device_id=(target, slab), device_id_type=MESH)

    def send_grad(k, carry):
        grad_copy(k).start()
        return carry

    lax.fori_loop(1, nchan, send_grad, 0)

    def share_copy(k):
        return pltpu.make_async_remote_copy(
            src_ref=agb.at[slab], dst_ref=agb.at[slab],
            send_sem=ag_send, recv_sem=ag_recv, device_id=(me, lax.rem(slab + k, ns)), device_id_type=MESH)

    def send_share(k, carry):
        share_copy(k).start()
        return carry

    @pl.when(slab < owners)
    def _():
        pltpu.make_async_copy(rsb, rsb, rs_recv).wait()
        total = kgs[pl.ds(slab * tp, tp)].astype(F32)
        for k in range(ns - 1):
            total = total + rsb[k].astype(F32)
        kgown[...] = total
        agb[slab] = total.astype(BF16)
        lax.fori_loop(1, ns, send_share, 0)

    pltpu.make_async_copy(igr, igr, ig_recv).wait()
    for q in range(8):
        total = igs[me, q].astype(F32)
        for k in range(nchan - 1):
            total = total + igr[k, q].astype(F32)
        for k in range(2):
            ig_ref[pl.ds((q // 4) * 8 + 2 * (q % 4) + k, CB, stride=16), :] = total[CB * k : CB * k + CB]

    @pl.when(slab < owners)
    def _():
        some = agb.at[pl.ds(0, owners - 1)]
        pltpu.make_async_copy(some, some, ag_recv).wait()

    @pl.when(slab >= owners)
    def _():
        some = agb.at[pl.ds(0, owners)]
        pltpu.make_async_copy(some, some, ag_recv).wait()

    kg_ref[...] = agb[...].reshape(owners * tp, FB, chans)[:27].astype(F32)

    for copy in sent:
        copy.wait_send()

    @pl.when(slab < ns - 1)
    def _():
        up_halo.wait_send()
        up_delta.wait_send()

    @pl.when(slab > 0)
    def _():
        down_halo.wait_send()
        down_delta.wait_send()

    @pl.when(slab < owners)
    def _():
        some = agb.at[pl.ds(0, owners - 1)]
        pltpu.make_async_copy(some, some, rs_send).wait()
        pltpu.make_async_copy(rsb, rsb, ag_send).wait()

    @pl.when(slab >= owners)
    def _():
        some = agb.at[pl.ds(0, owners)]
        pltpu.make_async_copy(some, some, rs_send).wait()

    pltpu.make_async_copy(igr, igr, ig_send).wait()


def device_call(grid, ns, tp, features, kernel, upstream):
    nyl, nxc = grid
    chips = nyl * nxc
    nchan = 2 * chips
    chans = nchan * CB
    owners = -(-27 // tp)
    out = pl.pallas_call(
        functools.partial(body, grid, ns, tp),
        out_shape=(
            jax.ShapeDtypeStruct((FB, 2, 8, NX), BF16),
            jax.ShapeDtypeStruct((CB * 16, NX), F32),
            jax.ShapeDtypeStruct((27, FB, chans), F32),
        ),
        in_specs=[pl.BlockSpec(memory_space=pl.ANY)] * 3,
        out_specs=[pl.BlockSpec(memory_space=pltpu.VMEM)] * 3,
        scratch_shapes=[
            pltpu.VMEM((CB, 2, 8, NX), BF16),
            pltpu.VMEM((27, FB, chans), BF16),
            pltpu.VMEM((FB, 2, 8, NX), BF16),
            pltpu.VMEM((CB * 16, NX), F32),
            pltpu.VMEM((FB * 16, NX), F32),
            pltpu.VMEM((nchan, 2, 8, 16, NX), BF16),
            pltpu.VMEM((4, 8, chans, NX), BF16),
            pltpu.VMEM((2, 2, 12 * FB, 2 * NX), F32),
            pltpu.VMEM((3, 12 * FB, 2 * chans), BF16),
            pltpu.VMEM((chans, 512), BF16),
            pltpu.VMEM((2, 8, FB, NX), BF16),
            pltpu.VMEM((2, 8, FB, NX), BF16),
            pltpu.VMEM((4, 10, 3 * FB, NX), BF16),
            pltpu.VMEM((owners * tp, FB, chans), BF16),
            pltpu.VMEM((ns - 1, tp, FB, chans), BF16),
            pltpu.VMEM((owners, tp, FB, chans), BF16),
            pltpu.VMEM((tp, FB, chans), F32),
            pltpu.VMEM((nchan, 8, 16, NX), BF16),
            pltpu.VMEM((nchan - 1, 8, 16, NX), BF16),
            pltpu.SemaphoreType.DMA((3,)),
            pltpu.SemaphoreType.DMA((2, chips)),
            pltpu.SemaphoreType.DMA((2, nchan)),
            pltpu.SemaphoreType.DMA((2, chips)),
            pltpu.SemaphoreType.DMA((2,)),
            pltpu.SemaphoreType.DMA((2,)),
            pltpu.SemaphoreType.DMA((2,)),
            pltpu.SemaphoreType.DMA((2,)),
            pltpu.SemaphoreType.DMA,
            pltpu.SemaphoreType.DMA,
            pltpu.SemaphoreType.DMA,
            pltpu.SemaphoreType.DMA,
            pltpu.SemaphoreType.DMA,
            pltpu.SemaphoreType.DMA,
        ],
        compiler_params=pltpu.CompilerParams(
            collective_id=0, has_side_effects=True, vmem_limit_bytes=32 * 1024 * 1024
        ),
    )(features, kernel, upstream)
    return out[0], out[1].reshape(CB, 2, 8, NX), out[2]


def solution(mesh):
    ns = mesh.shape["slab"]
    specs = (P("chan", "slab", None, None), P(None, "chan", None), P("chan", "slab", None, None))
    out_specs = (
        P("chan", "slab", None, None),
        P("chan", "slab", None, None),
        P(None, "chan", None),
    )
    call = functools.partial(device_call, (2, 4), ns, -(-27 // ns))
    return jax.shard_map(call, mesh=mesh, in_specs=specs, out_specs=out_specs, check_vma=False)
```

```python
import functools

import jax
import jax.numpy as jnp
from jax import lax
from jax.experimental import pallas as pl
from jax.experimental.pallas import tpu as pltpu
from jax.sharding import PartitionSpec as P

MESH = pl.DeviceIdType.MESH
F32 = jnp.float32
BF16 = jnp.bfloat16
CB = 8
FB = 16
NX = 128


def dot(a, b):
    return lax.dot_general(a, b, (((1,), (0,)), ((), ())), preferred_element_type=F32)


def dot_nt(a, b):
    return lax.dot_general(a, b, (((1,), (1,)), ((), ())), preferred_element_type=F32)


def shifted(v, lane):
    left = jnp.where(lane == NX - 1, 0.0, pltpu.roll(v, NX - 1, 1))
    right = jnp.where(lane == 0, 0.0, pltpu.roll(v, 1, 1))
    return left, right


def body(
    grid, tp,
    feat_hbm, kern_hbm, up_hbm,
    act_ref, ig_ref, kg_ref,
    feat, kern, up, rows_f, rows_u, land, xc, tacc, w4, wt, d1, dh, d3, kgs, rsb, agb, igs, igr,
    ring_sem, other_sem, in_sem, g_send, g_recv, f_send, h_send, h_recv, dh_send, dh_recv, rs_send, rs_recv, ag_send, ag_recv, ig_send, ig_recv,
):
    nyl, nxc, nyh, nz = grid
    ns = nyh * nz
    chips = nyl * nxc
    nchan = 2 * chips
    chans = nchan * CB
    owners = -(-27 // tp)
    reach = nz // 4
    me = lax.axis_index("chan")
    slab = lax.axis_index("slab")
    sz = lax.rem(slab, nz)
    sy = slab // nz
    core = lax.rem(me, 2)
    chip = me // 2
    cx = lax.rem(chip, nxc)
    cy = chip // nxc
    sib = chip * 2 + (1 - core)

    loads = [
        pltpu.make_async_copy(feat_hbm, feat, in_sem.at[0]),
        pltpu.make_async_copy(kern_hbm, kern, in_sem.at[1]),
        pltpu.make_async_copy(up_hbm, up, in_sem.at[2]),
    ]
    for load in loads:
        load.start()

    barrier = pltpu.get_barrier_semaphore()

    def slab_at(dy, dz):
        return lax.rem(sy + dy, nyh) * nz + lax.rem(sz + dz + nz, nz)

    def signal(semaphore, chan, target):
        pl.semaphore_signal(semaphore, inc=1, device_id=(chan, target), device_id_type=MESH)

    near = [(0, d) for k in range(1, reach + 1) for d in (k, -k)] + [(1, 0)]
    for dy, dz in reversed(near):
        signal(barrier, me, slab_at(dy, dz))
    for k in range(1, nchan):
        signal(barrier, lax.rem(me + k, nchan), slab)

    @pl.when(slab == nz - 1)
    def _():
        signal(barrier, me, slab + 1)

    @pl.when(slab == nz)
    def _():
        signal(barrier, me, slab - 1)

    loads[0].wait()
    rows_f[...] = feat[...].astype(F32).reshape(CB * 16, NX)
    for z in range(2):
        for yp in range(4):
            pair = [rows_f[pl.ds(z * 8 + 2 * yp + k, CB, stride=16), :] for k in range(2)]
            land[me, 0, z * 4 + yp] = jnp.concatenate(pair, 0).astype(BF16)

    pl.semaphore_wait(barrier, nchan - 1 + len(near) + jnp.where((slab == nz - 1) | (slab == nz), 1, 0))

    signal(ring_sem, me, slab_at(0, reach))
    signal(ring_sem, me, slab_at(0, -reach))

    up_halo = pltpu.make_async_remote_copy(
        src_ref=land.at[me, 0, pl.ds(4, 4)], dst_ref=land.at[me, 1, pl.ds(0, 4)],
        send_sem=h_send.at[0], recv_sem=h_recv.at[0], device_id=(me, slab + 1), device_id_type=MESH)
    down_halo = pltpu.make_async_remote_copy(
        src_ref=land.at[me, 0, pl.ds(0, 4)], dst_ref=land.at[me, 1, pl.ds(4, 4)],
        send_sem=h_send.at[1], recv_sem=h_recv.at[1], device_id=(me, slab - 1), device_id_type=MESH)

    @pl.when(slab < ns - 1)
    def _():
        up_halo.start()

    @pl.when(slab > 0)
    def _():
        down_halo.start()

    hops = [(j, k) for j in range(nyl) for k in range(nxc)][1:]

    def peer(j, k):
        return (lax.rem(cy + j, nyl) * nxc + lax.rem(cx + k, nxc)) * 2 + core

    def source(j, k):
        return (lax.rem(cy + nyl - j, nyl) * nxc + lax.rem(cx + nxc - k, nxc)) * 2 + core

    def gather_copy(part, holder, target, send_sem):
        return pltpu.make_async_remote_copy(
            src_ref=land.at[holder, part], dst_ref=land.at[holder, part],
            send_sem=send_sem, recv_sem=g_recv.at[part, holder], device_id=(target, slab), device_id_type=MESH)

    sent = []

    def send_own(part):
        for n, (j, k) in enumerate(hops):
            copy = gather_copy(part, me, peer(j, k), g_send.at[part, n])
            copy.start()
            sent.append(copy)
        copy = gather_copy(part, me, sib, g_send.at[part, chips - 1])
        copy.start()
        sent.append(copy)

    def forward(part):
        for n, (j, k) in enumerate(hops):
            holder = source(j, k)
            copy = gather_copy(part, holder, sib, f_send.at[part, n])
            copy.wait_recv()
            copy.start()
            sent.append(copy)

    def receive_rest(part):
        for q in range(chips):
            holder = lax.rem(chip + q, chips) * 2 + (1 - core)
            gather_copy(part, holder, sib, f_send.at[part, 0]).wait_recv()

    send_own(0)

    loads[1].wait()
    for a in range(3):
        taps = [kern[pl.ds(9 * a + 3 * b, 3)].reshape(3 * FB, chans) for b in range(3)]
        zero = jnp.zeros((3 * FB, chans), BF16)
        w4[a] = jnp.concatenate(
            [
                jnp.concatenate([taps[2], zero], 1),
                jnp.concatenate([taps[1], taps[2]], 1),
                jnp.concatenate([taps[0], taps[1]], 1),
                jnp.concatenate([zero, taps[0]], 1),
            ],
            0,
        )
    d3[...] = jnp.zeros(d3.shape, BF16)

    @pl.when(slab == 0)
    def _():
        land[me, 1, pl.ds(0, 4)] = jnp.zeros((4, 16, NX), BF16)

    @pl.when(slab == ns - 1)
    def _():
        land[me, 1, pl.ds(4, 4)] = jnp.zeros((4, 16, NX), BF16)

    @pl.when(slab > 0)
    def _():
        up_halo.wait_recv()

    @pl.when(slab < ns - 1)
    def _():
        down_halo.wait_recv()

    send_own(1)

    pl.semaphore_wait(ring_sem, 2)
    signal(other_sem, me, slab_at(1, 0))

    flipped = [kern[9 * a + 3 * b + e].astype(F32) for a in (2, 1, 0) for b in (2, 1, 0) for e in range(3)]
    flipped += [jnp.zeros((FB, chans), F32)] * 5
    for q in range(4):
        wt[:, pl.ds(q * 128, 128)] = jnp.transpose(jnp.concatenate(flipped[8 * q : 8 * q + 8], 0)).astype(BF16)

    loads[2].wait()
    rows_u[...] = up[...].astype(F32).reshape(FB * 16, NX)

    def unpack(part):
        for zi in range(2):
            z = (1, 2)[zi] if part == 0 else (0, 3)[zi]
            for yp in range(4):
                tiles = land[:, part, zi * 4 + yp].astype(F32)
                for k in range(2):
                    xc[z, 2 * yp + k] = tiles[:, CB * k : CB * k + CB].reshape(chans, NX).astype(BF16)

    def pair_rows(z, yp):
        return xc[z, pl.ds(2 * yp, 2)].reshape(2 * chans, NX)

    forward(0)
    receive_rest(0)
    unpack(0)
    for o in range(2):
        weights = jnp.concatenate([w4[1 - o], w4[2 - o]], 1)
        for q in range(2):
            cells = jnp.concatenate(
                [jnp.concatenate([pair_rows(z, 2 * q + k) for z in (1, 2)], 0) for k in range(2)], 1)
            tacc[o, q] = dot(weights, cells)

    forward(1)
    receive_rest(1)
    unpack(1)
    for o in range(2):
        for q in range(2):
            cells = jnp.concatenate([pair_rows(3 * o, 2 * q + k) for k in range(2)], 1)
            tacc[o, q] += dot(w4[2 * o], cells)

    lane = lax.broadcasted_iota(jnp.int32, (FB, NX), 1)

    def pair_sum(o, yp, yo):
        return tacc[o, yp // 2, pl.ds(yo * 3 * FB, 3 * FB), pl.ds((yp % 2) * NX, NX)]

    acts = []
    for o in range(2):
        for y in range(8):
            yp, r = y // 2, y % 2
            total = pair_sum(o, yp, 1 + r)
            if r == 0 and yp > 0:
                total = total + pair_sum(o, yp - 1, 3)
            if r == 1 and yp < 3:
                total = total + pair_sum(o, yp + 1, 0)
            from_left = shifted(total[0:FB], lane)[1]
            from_right = shifted(total[2 * FB : 3 * FB], lane)[0]
            pre = total[FB : 2 * FB] + from_left + from_right
            s = 1.0 / (1.0 + jnp.exp(-jnp.maximum(pre, -88.0)))
            upstream = rows_u[pl.ds(o * 8 + y, FB, stride=16), :]
            delta = (upstream * s * (1.0 + pre * (1.0 - s))).astype(BF16)
            rows_u[pl.ds(o * 8 + y, FB, stride=16), :] = pre * s
            d1[o, y] = delta
            left, right = shifted(delta.astype(F32), lane)
            d3[1 + o, 1 + y] = jnp.concatenate([left.astype(BF16), delta, right.astype(BF16)], 0)

    up_delta = pltpu.make_async_remote_copy(
        src_ref=d1.at[1], dst_ref=dh.at[0],
        send_sem=dh_send.at[0], recv_sem=dh_recv.at[0], device_id=(me, slab + 1), device_id_type=MESH)
    down_delta = pltpu.make_async_remote_copy(
        src_ref=d1.at[0], dst_ref=dh.at[1],
        send_sem=dh_send.at[1], recv_sem=dh_recv.at[1], device_id=(me, slab - 1), device_id_type=MESH)

    @pl.when(slab < ns - 1)
    def _():
        up_delta.start()

    @pl.when(slab > 0)
    def _():
        down_delta.start()

    for a in range(3):
        lhs = jnp.concatenate(
            [d3[1 + o, pl.ds(2 * yp, 4)].reshape(12 * FB, NX) for o in range(2) for yp in range(4)], 1)
        rhs = jnp.concatenate([pair_rows(o + a, yp) for o in range(2) for yp in range(4)], 1)
        g = dot_nt(lhs, rhs)
        for b in range(3):
            term = (
                g[(2 - b) * 3 * FB : (3 - b) * 3 * FB, :chans] + g[(3 - b) * 3 * FB : (4 - b) * 3 * FB, chans:]
            )
            kgs[pl.ds(9 * a + 3 * b, 3)] = term.reshape(3, FB, chans).astype(BF16)

    far = [(dy, dz) for dy in range(nyh) for dz in range(1 - nz // 2, nz // 2 + 1) if dy or dz]
    far.sort(key=lambda t: -abs(t[1]) - 2 * t[0])
    pl.semaphore_wait(other_sem, 1)
    for n, (dy, dz) in enumerate(far):
        owner = slab_at(dy, dz)
        term = pltpu.make_async_remote_copy(
            src_ref=kgs.at[pl.ds(lax.rem(owner, owners) * tp, tp)], dst_ref=rsb.at[n],
            send_sem=rs_send, recv_sem=rs_recv, device_id=(me, owner), device_id_type=MESH)

        @pl.when(owner < owners)
        def _():
            term.start()

    act_ref[...] = rows_u[...].reshape(FB, 2, 8, NX).astype(BF16)

    def place_halo(plane, z):
        for y in range(8):
            delta = dh[plane, y]
            left, right = shifted(delta.astype(F32), lane)
            d3[z, 1 + y] = jnp.concatenate([left.astype(BF16), delta, right.astype(BF16)], 0)

    @pl.when(slab > 0)
    def _():
        up_delta.wait_recv()
        place_halo(0, 0)

    @pl.when(slab < ns - 1)
    def _():
        down_delta.wait_recv()
        place_halo(1, 3)

    blank = jnp.zeros((80, 2 * NX), BF16)
    for o in range(2):
        for yp in range(4):
            cells = jnp.concatenate(
                [
                    jnp.concatenate(
                        [d3[o + z, pl.ds(2 * yp + k, 3)].reshape(9 * FB, NX) for z in range(3)], 0)
                    for k in range(2)
                ],
                1,
            )
            grad = dot(wt[...], jnp.concatenate([cells, blank], 0)).reshape(nchan, CB, 2 * NX)
            igs[:, o * 4 + yp] = jnp.concatenate([grad[:, :, :NX], grad[:, :, NX:]], 1).astype(BF16)

    def grad_copy(k):
        target = lax.rem(me + k, nchan)
        return pltpu.make_async_remote_copy(
            src_ref=igs.at[target], dst_ref=igr.at[k - 1],
            send_sem=ig_send, recv_sem=ig_recv, device_id=(target, slab), device_id_type=MESH)

    def send_grad(k, carry):
        grad_copy(k).start()
        return carry

    lax.fori_loop(1, nchan, send_grad, 0)

    @pl.when(slab < owners)
    def _():
        pltpu.make_async_copy(rsb, rsb, rs_recv).wait()
        total = kgs[pl.ds(slab * tp, tp)].astype(F32)
        for k in range(ns - 1):
            total = total + rsb[k].astype(F32)
        agb[slab] = total.astype(BF16)
        for dy, dz in far:
            pltpu.make_async_remote_copy(
                src_ref=agb.at[slab], dst_ref=agb.at[slab],
                send_sem=ag_send, recv_sem=ag_recv, device_id=(me, slab_at(dy, dz)), device_id_type=MESH).start()

    pltpu.make_async_copy(igr, igr, ig_recv).wait()
    for q in range(8):
        total = igs[me, q].astype(F32)
        for k in range(nchan - 1):
            total = total + igr[k, q].astype(F32)
        for k in range(2):
            ig_ref[pl.ds((q // 4) * 8 + 2 * (q % 4) + k, CB, stride=16), :] = total[CB * k : CB * k + CB]

    @pl.when(slab < owners)
    def _():
        some = agb.at[pl.ds(0, owners - 1)]
        pltpu.make_async_copy(some, some, ag_recv).wait()

    @pl.when(slab >= owners)
    def _():
        some = agb.at[pl.ds(0, owners)]
        pltpu.make_async_copy(some, some, ag_recv).wait()

    kg_ref[...] = agb[...].reshape(owners * tp, FB, chans)[:27].astype(F32)

    for copy in sent:
        copy.wait_send()

    @pl.when(slab < ns - 1)
    def _():
        up_halo.wait_send()
        up_delta.wait_send()

    @pl.when(slab > 0)
    def _():
        down_halo.wait_send()
        down_delta.wait_send()

    @pl.when(slab < owners)
    def _():
        some = agb.at[pl.ds(0, owners - 1)]
        pltpu.make_async_copy(some, some, rs_send).wait()
        pltpu.make_async_copy(rsb, rsb, ag_send).wait()

    @pl.when(slab >= owners)
    def _():
        some = agb.at[pl.ds(0, owners)]
        pltpu.make_async_copy(some, some, rs_send).wait()

    pltpu.make_async_copy(igr, igr, ig_send).wait()


def write_out(act, ig, kg, act_hbm, ig_hbm, kg_hbm, sem):
    copies = [
        pltpu.make_async_copy(act, act_hbm, sem.at[0]),
        pltpu.make_async_copy(ig, ig_hbm, sem.at[1]),
        pltpu.make_async_copy(kg, kg_hbm, sem.at[2]),
    ]
    for copy in copies:
        copy.start()
    for copy in copies:
        copy.wait()


def device_call(grid, tp, features, kernel, upstream):
    nyl, nxc, nyh, nz = grid
    ns = nyh * nz
    chips = nyl * nxc
    nchan = 2 * chips
    chans = nchan * CB
    owners = -(-27 // tp)
    shapes = (((FB, 2, 8, NX), BF16), ((CB * 16, NX), F32), ((27, FB, chans), F32))
    features, kernel, upstream = (
        pltpu.with_memory_space_constraint(v, pltpu.HBM) for v in (features, kernel, upstream)
    )
    out = pl.pallas_call(
        functools.partial(body, grid, tp),
        out_shape=tuple(pltpu.VMEM(*s) for s in shapes),
        in_specs=[pl.BlockSpec(memory_space=pltpu.HBM)] * 3,
        out_specs=[pl.BlockSpec(memory_space=pltpu.VMEM)] * 3,
        scratch_shapes=[
            pltpu.VMEM((CB, 2, 8, NX), BF16),
            pltpu.VMEM((27, FB, chans), BF16),
            pltpu.VMEM((FB, 2, 8, NX), BF16),
            pltpu.VMEM((CB * 16, NX), F32),
            pltpu.VMEM((FB * 16, NX), F32),
            pltpu.VMEM((nchan, 2, 8, 16, NX), BF16),
            pltpu.VMEM((4, 8, chans, NX), BF16),
            pltpu.VMEM((2, 2, 12 * FB, 2 * NX), F32),
            pltpu.VMEM((3, 12 * FB, 2 * chans), BF16),
            pltpu.VMEM((chans, 512), BF16),
            pltpu.VMEM((2, 8, FB, NX), BF16),
            pltpu.VMEM((2, 8, FB, NX), BF16),
            pltpu.VMEM((4, 10, 3 * FB, NX), BF16),
            pltpu.VMEM((owners * tp, FB, chans), BF16),
            pltpu.VMEM((ns - 1, tp, FB, chans), BF16),
            pltpu.VMEM((owners, tp, FB, chans), BF16),
            pltpu.VMEM((nchan, 8, 16, NX), BF16),
            pltpu.VMEM((nchan - 1, 8, 16, NX), BF16),
            pltpu.SemaphoreType.REGULAR,
            pltpu.SemaphoreType.REGULAR,
            pltpu.SemaphoreType.DMA((3,)),
            pltpu.SemaphoreType.DMA((2, chips)),
            pltpu.SemaphoreType.DMA((2, nchan)),
            pltpu.SemaphoreType.DMA((2, chips)),
            pltpu.SemaphoreType.DMA((2,)),
            pltpu.SemaphoreType.DMA((2,)),
            pltpu.SemaphoreType.DMA((2,)),
            pltpu.SemaphoreType.DMA((2,)),
            pltpu.SemaphoreType.DMA,
            pltpu.SemaphoreType.DMA,
            pltpu.SemaphoreType.DMA,
            pltpu.SemaphoreType.DMA,
            pltpu.SemaphoreType.DMA,
            pltpu.SemaphoreType.DMA,
        ],
        compiler_params=pltpu.CompilerParams(
            collective_id=0, has_side_effects=True, vmem_limit_bytes=32 * 1024 * 1024
        ),
    )(features, kernel, upstream)
    out = pl.pallas_call(
        write_out,
        out_shape=tuple(pltpu.HBM(*s) for s in shapes),
        in_specs=[pl.BlockSpec(memory_space=pltpu.VMEM)] * 3,
        out_specs=[pl.BlockSpec(memory_space=pltpu.HBM)] * 3,
        scratch_shapes=[pltpu.SemaphoreType.DMA((3,))],
        compiler_params=pltpu.CompilerParams(vmem_limit_bytes=1024 * 1024),
    )(*out)
    return out[0], out[1].reshape(CB, 2, 8, NX), out[2]


def solution(mesh):
    ns = mesh.shape["slab"]
    specs = (P("chan", "slab", None, None), P(None, "chan", None), P("chan", "slab", None, None))
    out_specs = (
        P("chan", "slab", None, None),
        P("chan", "slab", None, None),
        P(None, "chan", None),
    )
    call = functools.partial(device_call, (2, 4, 2, ns // 2), -(-27 // ns))
    return jax.shard_map(call, mesh=mesh, in_specs=specs, out_specs=out_specs, check_vma=False)
```

```python
import functools

import jax
import jax.numpy as jnp
from jax import lax
from jax.experimental import pallas as pl
from jax.experimental.pallas import tpu as pltpu
from jax.sharding import PartitionSpec as P

MESH = pl.DeviceIdType.MESH
F32 = jnp.float32
BF16 = jnp.bfloat16
CB = 8
FB = 16
NX = 128


def dot(a, b):
    return lax.dot_general(a, b, (((1,), (0,)), ((), ())), preferred_element_type=F32)


def dot_nt(a, b):
    return lax.dot_general(a, b, (((1,), (1,)), ((), ())), preferred_element_type=F32)


def shifted(v, lane):
    left = jnp.where(lane == NX - 1, 0.0, pltpu.roll(v, NX - 1, 1))
    right = jnp.where(lane == 0, 0.0, pltpu.roll(v, 1, 1))
    return left, right


def body(
    grid, tp,
    feat_hbm, kern_hbm, up_hbm,
    act_ref, ig_ref, kg_ref,
    feat, kern, up, rows_f, rows_u, land, xc, tacc, w4, wt, d1, dh, d3, kgs, rsb, agb, igs, igr,
    ring_sem, other_sem, in_sem, g_send, g_recv, f_send, h_send, h_recv, dh_send, dh_recv, rs_send, rs_recv, ag_send, ag_recv, ig_send, ig_recv,
):
    nyl, nxc, nyh, nz = grid
    ns = nyh * nz
    chips = nyl * nxc
    nchan = 2 * chips
    chans = nchan * CB
    owners = -(-27 // tp)
    reach = nz // 8
    me = lax.axis_index("chan")
    slab = lax.axis_index("slab")
    sz = lax.rem(slab, nz)
    sy = slab // nz
    core = lax.rem(me, 2)
    chip = me // 2
    cx = lax.rem(chip, nxc)
    cy = chip // nxc
    sib = chip * 2 + (1 - core)

    loads = [
        pltpu.make_async_copy(feat_hbm, feat, in_sem.at[0]),
        pltpu.make_async_copy(kern_hbm, kern, in_sem.at[1]),
        pltpu.make_async_copy(up_hbm, up, in_sem.at[2]),
    ]
    for load in loads:
        load.start()

    barrier = pltpu.get_barrier_semaphore()

    def slab_at(dy, dz):
        return lax.rem(sy + dy, nyh) * nz + lax.rem(sz + dz + nz, nz)

    def rank(t):
        return lax.rem(lax.rem(t, nz) + nz - nz * 9 // 16, nz) * nyh + t // nz

    place = rank(slab)

    def signal(semaphore, chan, target):
        pl.semaphore_signal(semaphore, inc=1, device_id=(chan, target), device_id_type=MESH)

    near = [(0, d) for k in range(1, reach + 1) for d in (k, -k)] + [(1, 0)]
    for dy, dz in reversed(near):
        signal(barrier, me, slab_at(dy, dz))
    for k in range(1, nchan):
        signal(barrier, lax.rem(me + k, nchan), slab)

    @pl.when(slab == nz - 1)
    def _():
        signal(barrier, me, slab + 1)

    @pl.when(slab == nz)
    def _():
        signal(barrier, me, slab - 1)

    loads[0].wait()
    rows_f[...] = feat[...].astype(F32).reshape(CB * 16, NX)
    for z in range(2):
        for yp in range(4):
            pair = [rows_f[pl.ds(z * 8 + 2 * yp + k, CB, stride=16), :] for k in range(2)]
            land[me, 0, z * 4 + yp] = jnp.concatenate(pair, 0).astype(BF16)

    pl.semaphore_wait(barrier, nchan - 1 + len(near) + jnp.where((slab == nz - 1) | (slab == nz), 1, 0))

    def tell(n):
        for d in (reach << n, -(reach << n)):
            signal(ring_sem.at[n], me, slab_at(0, d))

    tell(0)

    up_halo = pltpu.make_async_remote_copy(
        src_ref=land.at[me, 0, pl.ds(4, 4)], dst_ref=land.at[me, 1, pl.ds(0, 4)],
        send_sem=h_send.at[0], recv_sem=h_recv.at[0], device_id=(me, slab + 1), device_id_type=MESH)
    down_halo = pltpu.make_async_remote_copy(
        src_ref=land.at[me, 0, pl.ds(0, 4)], dst_ref=land.at[me, 1, pl.ds(4, 4)],
        send_sem=h_send.at[1], recv_sem=h_recv.at[1], device_id=(me, slab - 1), device_id_type=MESH)

    @pl.when(slab < ns - 1)
    def _():
        up_halo.start()

    @pl.when(slab > 0)
    def _():
        down_halo.start()

    hops = [(j, k) for j in range(nyl) for k in range(nxc)][1:]
    hops.sort(key=lambda t: -t[0] - min(t[1], nxc - t[1]))

    def peer(j, k):
        return (lax.rem(cy + j, nyl) * nxc + lax.rem(cx + k, nxc)) * 2 + core

    def source(j, k):
        return (lax.rem(cy + nyl - j, nyl) * nxc + lax.rem(cx + nxc - k, nxc)) * 2 + core

    def gather_copy(part, holder, target, send_sem):
        return pltpu.make_async_remote_copy(
            src_ref=land.at[holder, part], dst_ref=land.at[holder, part],
            send_sem=send_sem, recv_sem=g_recv.at[part, holder], device_id=(target, slab), device_id_type=MESH)

    sent = []

    def send_own(part):
        for n, (j, k) in enumerate(hops):
            copy = gather_copy(part, me, peer(j, k), g_send.at[part, n])
            copy.start()
            sent.append(copy)
        copy = gather_copy(part, me, sib, g_send.at[part, chips - 1])
        copy.start()
        sent.append(copy)

    def forward(part):
        for n, (j, k) in enumerate(hops):
            holder = source(j, k)
            copy = gather_copy(part, holder, sib, f_send.at[part, n])
            copy.wait_recv()
            copy.start()
            sent.append(copy)

    def receive_rest(part):
        for q in range(chips):
            holder = lax.rem(chip + q, chips) * 2 + (1 - core)
            gather_copy(part, holder, sib, f_send.at[part, 0]).wait_recv()

    send_own(0)

    loads[1].wait()
    for a in range(3):
        taps = [kern[pl.ds(9 * a + 3 * b, 3)].reshape(3 * FB, chans) for b in range(3)]
        zero = jnp.zeros((3 * FB, chans), BF16)
        w4[a] = jnp.concatenate(
            [
                jnp.concatenate([taps[2], zero], 1),
                jnp.concatenate([taps[1], taps[2]], 1),
                jnp.concatenate([taps[0], taps[1]], 1),
                jnp.concatenate([zero, taps[0]], 1),
            ],
            0,
        )
    d3[...] = jnp.zeros(d3.shape, BF16)

    @pl.when(slab == 0)
    def _():
        land[me, 1, pl.ds(0, 4)] = jnp.zeros((4, 16, NX), BF16)

    @pl.when(slab == ns - 1)
    def _():
        land[me, 1, pl.ds(4, 4)] = jnp.zeros((4, 16, NX), BF16)

    @pl.when(slab > 0)
    def _():
        up_halo.wait_recv()

    @pl.when(slab < ns - 1)
    def _():
        down_halo.wait_recv()

    send_own(1)
    pl.semaphore_wait(ring_sem.at[0], 2)
    tell(1)

    flipped = [kern[9 * a + 3 * b + e].astype(F32) for a in (2, 1, 0) for b in (2, 1, 0) for e in range(3)]
    flipped += [jnp.zeros((FB, chans), F32)] * 5
    for q in range(4):
        wt[:, pl.ds(q * 128, 128)] = jnp.transpose(jnp.concatenate(flipped[8 * q : 8 * q + 8], 0)).astype(BF16)

    loads[2].wait()
    rows_u[...] = up[...].astype(F32).reshape(FB * 16, NX)

    def unpack(part):
        for zi in range(2):
            z = (1, 2)[zi] if part == 0 else (0, 3)[zi]
            for yp in range(4):
                tiles = land[:, part, zi * 4 + yp].astype(F32)
                for k in range(2):
                    xc[z, 2 * yp + k] = tiles[:, CB * k : CB * k + CB].reshape(chans, NX).astype(BF16)

    def pair_rows(z, yp):
        return xc[z, pl.ds(2 * yp, 2)].reshape(2 * chans, NX)

    forward(0)
    pl.semaphore_wait(ring_sem.at[1], 2)
    signal(other_sem, me, slab_at(1, 0))
    receive_rest(0)
    unpack(0)
    for o in range(2):
        weights = jnp.concatenate([w4[1 - o], w4[2 - o]], 1)
        for q in range(2):
            cells = jnp.concatenate(
                [jnp.concatenate([pair_rows(z, 2 * q + k) for z in (1, 2)], 0) for k in range(2)], 1)
            tacc[o, q] = dot(weights, cells)

    forward(1)
    receive_rest(1)
    unpack(1)
    for o in range(2):
        for q in range(2):
            cells = jnp.concatenate([pair_rows(3 * o, 2 * q + k) for k in range(2)], 1)
            tacc[o, q] += dot(w4[2 * o], cells)

    lane = lax.broadcasted_iota(jnp.int32, (FB, NX), 1)

    def pair_sum(o, yp, yo):
        return tacc[o, yp // 2, pl.ds(yo * 3 * FB, 3 * FB), pl.ds((yp % 2) * NX, NX)]

    acts = []
    for o in range(2):
        for y in range(8):
            yp, r = y // 2, y % 2
            total = pair_sum(o, yp, 1 + r)
            if r == 0 and yp > 0:
                total = total + pair_sum(o, yp - 1, 3)
            if r == 1 and yp < 3:
                total = total + pair_sum(o, yp + 1, 0)
            from_left = shifted(total[0:FB], lane)[1]
            from_right = shifted(total[2 * FB : 3 * FB], lane)[0]
            pre = total[FB : 2 * FB] + from_left + from_right
            s = 1.0 / (1.0 + jnp.exp(-jnp.maximum(pre, -88.0)))
            upstream = rows_u[pl.ds(o * 8 + y, FB, stride=16), :]
            delta = (upstream * s * (1.0 + pre * (1.0 - s))).astype(BF16)
            rows_u[pl.ds(o * 8 + y, FB, stride=16), :] = pre * s
            d1[o, y] = delta
            left, right = shifted(delta.astype(F32), lane)
            d3[1 + o, 1 + y] = jnp.concatenate([left.astype(BF16), delta, right.astype(BF16)], 0)

    up_delta = pltpu.make_async_remote_copy(
        src_ref=d1.at[1], dst_ref=dh.at[0],
        send_sem=dh_send.at[0], recv_sem=dh_recv.at[0], device_id=(me, slab + 1), device_id_type=MESH)
    down_delta = pltpu.make_async_remote_copy(
        src_ref=d1.at[0], dst_ref=dh.at[1],
        send_sem=dh_send.at[1], recv_sem=dh_recv.at[1], device_id=(me, slab - 1), device_id_type=MESH)

    @pl.when(slab < ns - 1)
    def _():
        up_delta.start()

    @pl.when(slab > 0)
    def _():
        down_delta.start()

    for a in range(3):
        lhs = jnp.concatenate(
            [d3[1 + o, pl.ds(2 * yp, 4)].reshape(12 * FB, NX) for o in range(2) for yp in range(4)], 1)
        rhs = jnp.concatenate([pair_rows(o + a, yp) for o in range(2) for yp in range(4)], 1)
        g = dot_nt(lhs, rhs)
        for b in range(3):
            term = (
                g[(2 - b) * 3 * FB : (3 - b) * 3 * FB, :chans] + g[(3 - b) * 3 * FB : (4 - b) * 3 * FB, chans:]
            )
            kgs[pl.ds(9 * a + 3 * b, 3)] = term.reshape(3, FB, chans).astype(BF16)

    far = [(dy, dz) for dy in range(nyh) for dz in range(1 - nz // 2, nz // 2 + 1) if dy or dz]
    far.sort(key=lambda t: -abs(t[1]) - 2 * t[0])
    pl.semaphore_wait(other_sem, 1)
    for n, (dy, dz) in enumerate(far):
        owner = slab_at(dy, dz)
        term = pltpu.make_async_remote_copy(
            src_ref=kgs.at[pl.ds(lax.rem(rank(owner), owners) * tp, tp)], dst_ref=rsb.at[n],
            send_sem=rs_send, recv_sem=rs_recv, device_id=(me, owner), device_id_type=MESH)

        @pl.when(rank(owner) < owners)
        def _():
            term.start()

    act_ref[...] = rows_u[...].reshape(FB, 2, 8, NX).astype(BF16)

    def place_halo(plane, z):
        for y in range(8):
            delta = dh[plane, y]
            left, right = shifted(delta.astype(F32), lane)
            d3[z, 1 + y] = jnp.concatenate([left.astype(BF16), delta, right.astype(BF16)], 0)

    @pl.when(slab > 0)
    def _():
        up_delta.wait_recv()
        place_halo(0, 0)

    @pl.when(slab < ns - 1)
    def _():
        down_delta.wait_recv()
        place_halo(1, 3)

    blank = jnp.zeros((80, 2 * NX), BF16)
    for o in range(2):
        for yp in range(4):
            cells = jnp.concatenate(
                [
                    jnp.concatenate(
                        [d3[o + z, pl.ds(2 * yp + k, 3)].reshape(9 * FB, NX) for z in range(3)], 0)
                    for k in range(2)
                ],
                1,
            )
            grad = dot(wt[...], jnp.concatenate([cells, blank], 0)).reshape(nchan, CB, 2 * NX)
            igs[:, o * 4 + yp] = jnp.concatenate([grad[:, :, :NX], grad[:, :, NX:]], 1).astype(BF16)

    def grad_copy(k):
        target = lax.rem(me + k, nchan)
        return pltpu.make_async_remote_copy(
            src_ref=igs.at[target], dst_ref=igr.at[k - 1],
            send_sem=ig_send, recv_sem=ig_recv, device_id=(target, slab), device_id_type=MESH)

    def send_grad(k, carry):
        grad_copy(k).start()
        return carry

    lax.fori_loop(1, nchan, send_grad, 0)

    @pl.when(place < owners)
    def _():
        pltpu.make_async_copy(rsb, rsb, rs_recv).wait()
        total = kgs[pl.ds(place * tp, tp)].astype(F32)
        for k in range(ns - 1):
            total = total + rsb[k].astype(F32)
        agb[place] = total.astype(BF16)
        for target in sorted(range(ns), key=lambda t: min(t % nz, nz - t % nz)):
            share = pltpu.make_async_remote_copy(
                src_ref=agb.at[place], dst_ref=agb.at[place],
                send_sem=ag_send, recv_sem=ag_recv, device_id=(me, target), device_id_type=MESH)

            @pl.when(slab != target)
            def _():
                share.start()

    pltpu.make_async_copy(igr, igr, ig_recv).wait()
    for q in range(8):
        total = igs[me, q].astype(F32)
        for k in range(nchan - 1):
            total = total + igr[k, q].astype(F32)
        for k in range(2):
            ig_ref[pl.ds((q // 4) * 8 + 2 * (q % 4) + k, CB, stride=16), :] = total[CB * k : CB * k + CB]

    @pl.when(place < owners)
    def _():
        some = agb.at[pl.ds(0, owners - 1)]
        pltpu.make_async_copy(some, some, ag_recv).wait()

    @pl.when(place >= owners)
    def _():
        some = agb.at[pl.ds(0, owners)]
        pltpu.make_async_copy(some, some, ag_recv).wait()

    kg_ref[...] = agb[...].reshape(owners * tp, FB, chans)[:27].astype(F32)

    for copy in sent:
        copy.wait_send()

    @pl.when(slab < ns - 1)
    def _():
        up_halo.wait_send()
        up_delta.wait_send()

    @pl.when(slab > 0)
    def _():
        down_halo.wait_send()
        down_delta.wait_send()

    @pl.when(place < owners)
    def _():
        some = agb.at[pl.ds(0, owners - 1)]
        pltpu.make_async_copy(some, some, rs_send).wait()
        pltpu.make_async_copy(rsb, rsb, ag_send).wait()

    @pl.when(place >= owners)
    def _():
        some = agb.at[pl.ds(0, owners)]
        pltpu.make_async_copy(some, some, rs_send).wait()

    pltpu.make_async_copy(igr, igr, ig_send).wait()


def write_out(act, ig, kg, act_hbm, ig_hbm, kg_hbm, sem):
    copies = [
        pltpu.make_async_copy(act, act_hbm, sem.at[0]),
        pltpu.make_async_copy(ig, ig_hbm, sem.at[1]),
        pltpu.make_async_copy(kg, kg_hbm, sem.at[2]),
    ]
    for copy in copies:
        copy.start()
    for copy in copies:
        copy.wait()


def device_call(grid, tp, features, kernel, upstream):
    nyl, nxc, nyh, nz = grid
    ns = nyh * nz
    chips = nyl * nxc
    nchan = 2 * chips
    chans = nchan * CB
    owners = -(-27 // tp)
    shapes = (((FB, 2, 8, NX), BF16), ((CB * 16, NX), F32), ((27, FB, chans), F32))
    features, kernel, upstream = (
        pltpu.with_memory_space_constraint(v, pltpu.HBM) for v in (features, kernel, upstream)
    )
    out = pl.pallas_call(
        functools.partial(body, grid, tp),
        out_shape=tuple(pltpu.VMEM(*s) for s in shapes),
        in_specs=[pl.BlockSpec(memory_space=pltpu.HBM)] * 3,
        out_specs=[pl.BlockSpec(memory_space=pltpu.VMEM)] * 3,
        scratch_shapes=[
            pltpu.VMEM((CB, 2, 8, NX), BF16),
            pltpu.VMEM((27, FB, chans), BF16),
            pltpu.VMEM((FB, 2, 8, NX), BF16),
            pltpu.VMEM((CB * 16, NX), F32),
            pltpu.VMEM((FB * 16, NX), F32),
            pltpu.VMEM((nchan, 2, 8, 16, NX), BF16),
            pltpu.VMEM((4, 8, chans, NX), BF16),
            pltpu.VMEM((2, 2, 12 * FB, 2 * NX), F32),
            pltpu.VMEM((3, 12 * FB, 2 * chans), BF16),
            pltpu.VMEM((chans, 512), BF16),
            pltpu.VMEM((2, 8, FB, NX), BF16),
            pltpu.VMEM((2, 8, FB, NX), BF16),
            pltpu.VMEM((4, 10, 3 * FB, NX), BF16),
            pltpu.VMEM((owners * tp, FB, chans), BF16),
            pltpu.VMEM((ns - 1, tp, FB, chans), BF16),
            pltpu.VMEM((owners, tp, FB, chans), BF16),
            pltpu.VMEM((nchan, 8, 16, NX), BF16),
            pltpu.VMEM((nchan - 1, 8, 16, NX), BF16),
            pltpu.SemaphoreType.REGULAR((2,)),
            pltpu.SemaphoreType.REGULAR,
            pltpu.SemaphoreType.DMA((3,)),
            pltpu.SemaphoreType.DMA((2, chips)),
            pltpu.SemaphoreType.DMA((2, nchan)),
            pltpu.SemaphoreType.DMA((2, chips)),
            pltpu.SemaphoreType.DMA((2,)),
            pltpu.SemaphoreType.DMA((2,)),
            pltpu.SemaphoreType.DMA((2,)),
            pltpu.SemaphoreType.DMA((2,)),
            pltpu.SemaphoreType.DMA,
            pltpu.SemaphoreType.DMA,
            pltpu.SemaphoreType.DMA,
            pltpu.SemaphoreType.DMA,
            pltpu.SemaphoreType.DMA,
            pltpu.SemaphoreType.DMA,
        ],
        compiler_params=pltpu.CompilerParams(
            collective_id=0, has_side_effects=True, vmem_limit_bytes=32 * 1024 * 1024
        ),
    )(features, kernel, upstream)
    out = pl.pallas_call(
        write_out,
        out_shape=tuple(pltpu.HBM(*s) for s in shapes),
        in_specs=[pl.BlockSpec(memory_space=pltpu.VMEM)] * 3,
        out_specs=[pl.BlockSpec(memory_space=pltpu.HBM)] * 3,
        scratch_shapes=[pltpu.SemaphoreType.DMA((3,))],
        compiler_params=pltpu.CompilerParams(vmem_limit_bytes=1024 * 1024),
    )(*out)
    return out[0], out[1].reshape(CB, 2, 8, NX), out[2]


def solution(mesh):
    ns = mesh.shape["slab"]
    specs = (P("chan", "slab", None, None), P(None, "chan", None), P("chan", "slab", None, None))
    out_specs = (
        P("chan", "slab", None, None),
        P("chan", "slab", None, None),
        P(None, "chan", None),
    )
    call = functools.partial(device_call, (2, 4, 2, ns // 2), -(-27 // ns))
    return jax.shard_map(call, mesh=mesh, in_specs=specs, out_specs=out_specs, check_vma=False)
```

```python
import functools

import jax
import jax.numpy as jnp
from jax import lax
from jax.experimental import pallas as pl
from jax.experimental.pallas import tpu as pltpu
from jax.sharding import PartitionSpec as P

MESH = pl.DeviceIdType.MESH
F32 = jnp.float32
BF16 = jnp.bfloat16
CB = 8
FB = 16
NX = 128


def dot(a, b):
    return lax.dot_general(a, b, (((1,), (0,)), ((), ())), preferred_element_type=F32)


def dot_nt(a, b):
    return lax.dot_general(a, b, (((1,), (1,)), ((), ())), preferred_element_type=F32)


def shifted(v, lane):
    left = jnp.where(lane == NX - 1, 0.0, pltpu.roll(v, NX - 1, 1))
    right = jnp.where(lane == 0, 0.0, pltpu.roll(v, 1, 1))
    return left, right


def body(
    grid,
    feat_hbm, kern_hbm, up_hbm,
    act_ref, ig_ref, kg_ref,
    feat, kern, up, rows_f, rows_u, land, xc, tacc, w4, wt, d1, dh, d3, kgs, rsb, agb, igf, igx, igs, igr,
    ring_sem, other_sem, in_sem, g_send, g_recv, f_send, h_send, h_recv, dh_send, dh_recv, rs_send, rs_recv, ag_send, ag_recv, ig_send, ig_recv, pair_sem,
):
    nyl, nxc, nyh, nz = grid
    ns = nyh * nz
    chips = nyl * nxc
    nchan = 2 * chips
    chans = nchan * CB
    reach = nz // 8
    me = lax.axis_index("chan")
    slab = lax.axis_index("slab")
    sz = lax.rem(slab, nz)
    sy = slab // nz
    core = lax.rem(me, 2)
    chip = me // 2
    cx = lax.rem(chip, nxc)
    cy = chip // nxc
    sib = chip * 2 + (1 - core)

    loads = [
        pltpu.make_async_copy(feat_hbm, feat, in_sem.at[0]),
        pltpu.make_async_copy(kern_hbm, kern, in_sem.at[1]),
        pltpu.make_async_copy(up_hbm, up, in_sem.at[2]),
    ]
    for load in loads:
        load.start()

    barrier = pltpu.get_barrier_semaphore()

    def slab_at(dy, dz):
        return lax.rem(sy + dy, nyh) * nz + lax.rem(sz + dz + nz, nz)

    first = nz * 9 // 16
    turn = lax.rem(sz + nz - first, nz) * nyh + sy
    tap = 9 * lax.rem(turn, 3) + turn // 3

    def owner_of(t):
        place = 3 * (t % 9) + t // 9
        return (place % nyh) * nz + (place // nyh + first) % nz

    def signal(semaphore, chan, target):
        pl.semaphore_signal(semaphore, inc=1, device_id=(chan, target), device_id_type=MESH)

    hops = [(j, k) for j in range(nyl) for k in range(nxc)][1:]
    hops.sort(key=lambda t: -t[0] - min(t[1], nxc - t[1]))

    def peer(j, k):
        return (lax.rem(cy + j, nyl) * nxc + lax.rem(cx + k, nxc)) * 2 + core

    near = [(0, d) for k in range(1, reach + 1) for d in (k, -k)] + [(1, 0)]
    for dy, dz in reversed(near):
        signal(barrier, me, slab_at(dy, dz))
    for j, k in hops:
        for c in (core, 1 - core):
            signal(barrier, peer(j, k) + c - core, slab)
    signal(barrier, sib, slab)

    @pl.when(slab == nz - 1)
    def _():
        signal(barrier, me, slab + 1)

    @pl.when(slab == nz)
    def _():
        signal(barrier, me, slab - 1)

    loads[0].wait()
    rows_f[...] = feat[...].astype(F32).reshape(CB * 16, NX)
    for z in range(2):
        for yp in range(4):
            pair = [rows_f[pl.ds(z * 8 + 2 * yp + k, CB, stride=16), :] for k in range(2)]
            land[me, 0, z * 4 + yp] = jnp.concatenate(pair, 0).astype(BF16)

    pl.semaphore_wait(barrier, nchan - 1 + len(near) + jnp.where((slab == nz - 1) | (slab == nz), 1, 0))

    def tell(n):
        for d in (reach << n, -(reach << n)):
            signal(ring_sem.at[n], me, slab_at(0, d))

    tell(0)

    up_halo = pltpu.make_async_remote_copy(
        src_ref=land.at[me, 0, pl.ds(4, 4)], dst_ref=land.at[me, 1, pl.ds(0, 4)],
        send_sem=h_send.at[0], recv_sem=h_recv.at[0], device_id=(me, slab + 1), device_id_type=MESH)
    down_halo = pltpu.make_async_remote_copy(
        src_ref=land.at[me, 0, pl.ds(0, 4)], dst_ref=land.at[me, 1, pl.ds(4, 4)],
        send_sem=h_send.at[1], recv_sem=h_recv.at[1], device_id=(me, slab - 1), device_id_type=MESH)

    @pl.when(slab < ns - 1)
    def _():
        up_halo.start()

    @pl.when(slab > 0)
    def _():
        down_halo.start()

    def source(j, k):
        return (lax.rem(cy + nyl - j, nyl) * nxc + lax.rem(cx + nxc - k, nxc)) * 2 + core

    def gather_copy(part, holder, target, send_sem):
        return pltpu.make_async_remote_copy(
            src_ref=land.at[holder, part], dst_ref=land.at[holder, part],
            send_sem=send_sem, recv_sem=g_recv.at[part, holder], device_id=(target, slab), device_id_type=MESH)

    sent = []

    def send_own(part):
        for n, (j, k) in enumerate(hops):
            copy = gather_copy(part, me, peer(j, k), g_send.at[part, n])
            copy.start()
            sent.append(copy)
        copy = gather_copy(part, me, sib, g_send.at[part, chips - 1])
        copy.start()
        sent.append(copy)

    def forward(part):
        for n, (j, k) in enumerate(hops):
            holder = source(j, k)
            copy = gather_copy(part, holder, sib, f_send.at[part, n])
            copy.wait_recv()
            copy.start()
            sent.append(copy)

    def receive_rest(part):
        for q in range(chips):
            holder = lax.rem(chip + q, chips) * 2 + (1 - core)
            gather_copy(part, holder, sib, f_send.at[part, 0]).wait_recv()

    send_own(0)

    loads[1].wait()
    for a in range(3):
        taps = [kern[pl.ds(9 * a + 3 * b, 3)].reshape(3 * FB, chans) for b in range(3)]
        zero = jnp.zeros((3 * FB, chans), BF16)
        w4[a] = jnp.concatenate(
            [
                jnp.concatenate([taps[2], zero], 1),
                jnp.concatenate([taps[1], taps[2]], 1),
                jnp.concatenate([taps[0], taps[1]], 1),
                jnp.concatenate([zero, taps[0]], 1),
            ],
            0,
        )
    d3[...] = jnp.zeros(d3.shape, BF16)

    @pl.when(slab == 0)
    def _():
        land[me, 1, pl.ds(0, 4)] = jnp.zeros((4, 16, NX), BF16)

    @pl.when(slab == ns - 1)
    def _():
        land[me, 1, pl.ds(4, 4)] = jnp.zeros((4, 16, NX), BF16)

    @pl.when(slab > 0)
    def _():
        up_halo.wait_recv()

    @pl.when(slab < ns - 1)
    def _():
        down_halo.wait_recv()

    send_own(1)
    pl.semaphore_wait(ring_sem.at[0], 2)
    tell(1)

    flipped = [kern[9 * a + 3 * b + e].astype(F32) for a in (2, 1, 0) for b in (2, 1, 0) for e in range(3)]
    flipped += [jnp.zeros((FB, chans), F32)] * 5
    for q in range(4):
        wt[:, pl.ds(q * 128, 128)] = jnp.transpose(jnp.concatenate(flipped[8 * q : 8 * q + 8], 0)).astype(BF16)

    loads[2].wait()
    rows_u[...] = up[...].astype(F32).reshape(FB * 16, NX)

    def unpack(part):
        for zi in range(2):
            z = (1, 2)[zi] if part == 0 else (0, 3)[zi]
            for yp in range(4):
                tiles = land[:, part, zi * 4 + yp].astype(F32)
                for k in range(2):
                    xc[z, 2 * yp + k] = tiles[:, CB * k : CB * k + CB].reshape(chans, NX).astype(BF16)

    def pair_rows(z, yp):
        return xc[z, pl.ds(2 * yp, 2)].reshape(2 * chans, NX)

    forward(0)
    pl.semaphore_wait(ring_sem.at[1], 2)
    signal(other_sem, me, slab_at(1, 0))
    receive_rest(0)
    unpack(0)
    for o in range(2):
        weights = jnp.concatenate([w4[1 - o], w4[2 - o]], 1)
        for q in range(2):
            cells = jnp.concatenate(
                [jnp.concatenate([pair_rows(z, 2 * q + k) for z in (1, 2)], 0) for k in range(2)], 1)
            tacc[o, q] = dot(weights, cells)

    forward(1)
    receive_rest(1)
    unpack(1)
    for o in range(2):
        for q in range(2):
            cells = jnp.concatenate([pair_rows(3 * o, 2 * q + k) for k in range(2)], 1)
            tacc[o, q] += dot(w4[2 * o], cells)

    lane = lax.broadcasted_iota(jnp.int32, (FB, NX), 1)

    def pair_sum(o, yp, yo):
        return tacc[o, yp // 2, pl.ds(yo * 3 * FB, 3 * FB), pl.ds((yp % 2) * NX, NX)]

    acts = []
    for o in range(2):
        for y in range(8):
            yp, r = y // 2, y % 2
            total = pair_sum(o, yp, 1 + r)
            if r == 0 and yp > 0:
                total = total + pair_sum(o, yp - 1, 3)
            if r == 1 and yp < 3:
                total = total + pair_sum(o, yp + 1, 0)
            from_left = shifted(total[0:FB], lane)[1]
            from_right = shifted(total[2 * FB : 3 * FB], lane)[0]
            pre = total[FB : 2 * FB] + from_left + from_right
            s = 1.0 / (1.0 + jnp.exp(-jnp.maximum(pre, -88.0)))
            upstream = rows_u[pl.ds(o * 8 + y, FB, stride=16), :]
            delta = (upstream * s * (1.0 + pre * (1.0 - s))).astype(BF16)
            rows_u[pl.ds(o * 8 + y, FB, stride=16), :] = pre * s
            d1[o, y] = delta
            left, right = shifted(delta.astype(F32), lane)
            d3[1 + o, 1 + y] = jnp.concatenate([left.astype(BF16), delta, right.astype(BF16)], 0)

    up_delta = pltpu.make_async_remote_copy(
        src_ref=d1.at[1], dst_ref=dh.at[0],
        send_sem=dh_send.at[0], recv_sem=dh_recv.at[0], device_id=(me, slab + 1), device_id_type=MESH)
    down_delta = pltpu.make_async_remote_copy(
        src_ref=d1.at[0], dst_ref=dh.at[1],
        send_sem=dh_send.at[1], recv_sem=dh_recv.at[1], device_id=(me, slab - 1), device_id_type=MESH)

    @pl.when(slab < ns - 1)
    def _():
        up_delta.start()

    @pl.when(slab > 0)
    def _():
        down_delta.start()

    for a in range(3):
        lhs = jnp.concatenate(
            [d3[1 + o, pl.ds(2 * yp, 4)].reshape(12 * FB, NX) for o in range(2) for yp in range(4)], 1)
        rhs = jnp.concatenate([pair_rows(o + a, yp) for o in range(2) for yp in range(4)], 1)
        g = dot_nt(lhs, rhs)
        for b in range(3):
            term = (
                g[(2 - b) * 3 * FB : (3 - b) * 3 * FB, :chans] + g[(3 - b) * 3 * FB : (4 - b) * 3 * FB, chans:]
            )
            kgs[pl.ds(9 * a + 3 * b, 3)] = term.reshape(3, FB, chans).astype(BF16)
        if a == 0:
            pl.semaphore_wait(other_sem, 1)
        for t in range(9 * a, 9 * a + 9):
            send = pltpu.make_async_remote_copy(
                src_ref=kgs.at[t], dst_ref=rsb.at[slab],
                send_sem=rs_send, recv_sem=rs_recv, device_id=(me, owner_of(t)), device_id_type=MESH)

            @pl.when(slab != owner_of(t))
            def _():
                send.start()

    act_ref[...] = rows_u[...].reshape(FB, 2, 8, NX).astype(BF16)

    def place_halo(plane, z):
        for y in range(8):
            delta = dh[plane, y]
            left, right = shifted(delta.astype(F32), lane)
            d3[z, 1 + y] = jnp.concatenate([left.astype(BF16), delta, right.astype(BF16)], 0)

    @pl.when(slab > 0)
    def _():
        up_delta.wait_recv()
        place_halo(0, 0)

    @pl.when(slab < ns - 1)
    def _():
        down_delta.wait_recv()
        place_halo(1, 3)

    blank = jnp.zeros((80, 2 * NX), BF16)
    for o in range(2):
        for yp in range(4):
            cells = jnp.concatenate(
                [
                    jnp.concatenate(
                        [d3[o + z, pl.ds(2 * yp + k, 3)].reshape(9 * FB, NX) for z in range(3)], 0)
                    for k in range(2)
                ],
                1,
            )
            grad = dot(wt[...], jnp.concatenate([cells, blank], 0)).reshape(chips, 2, CB, 2 * NX)
            grad = jnp.concatenate([grad[..., :NX], grad[..., NX:]], 2)
            for c in range(2):
                igf[c, :, o * 4 + yp] = grad[:, c]

    pair_copy = pltpu.make_async_remote_copy(
        src_ref=igf.at[1 - core], dst_ref=igx,
        send_sem=pair_sem.at[0], recv_sem=pair_sem.at[1], device_id=(sib, slab), device_id_type=MESH)
    pair_copy.start()
    pair_copy.wait_recv()
    for q in range(chips):
        igs[q] = (igf[core, q] + igx[q]).astype(BF16)
    for n, (j, k) in enumerate(hops):
        target = peer(j, k)
        pltpu.make_async_remote_copy(
            src_ref=igs.at[target // 2], dst_ref=igr.at[n],
            send_sem=ig_send, recv_sem=ig_recv, device_id=(target, slab), device_id_type=MESH).start()

    others = rsb.at[pl.ds(0, ns - 1)]

    @pl.when(turn < 27)
    def _():
        rsb[slab] = kgs[tap]
        pltpu.make_async_copy(others, others, rs_recv).wait()
        total = rsb[0].astype(F32)
        for k in range(1, ns):
            total = total + rsb[k].astype(F32)
        agb[tap] = total.astype(BF16)
        for target in sorted(range(ns), key=lambda t: min(t % nz, nz - t % nz)):
            share = pltpu.make_async_remote_copy(
                src_ref=agb.at[tap], dst_ref=agb.at[tap],
                send_sem=ag_send, recv_sem=ag_recv, device_id=(me, target), device_id_type=MESH)

            @pl.when(slab != target)
            def _():
                share.start()

    pltpu.make_async_copy(igr, igr, ig_recv).wait()
    for q in range(8):
        total = igs[chip, q].astype(F32)
        for k in range(chips - 1):
            total = total + igr[k, q].astype(F32)
        for k in range(2):
            ig_ref[pl.ds((q // 4) * 8 + 2 * (q % 4) + k, CB, stride=16), :] = total[CB * k : CB * k + CB]

    @pl.when(turn < 27)
    def _():
        some = agb.at[pl.ds(0, 26)]
        pltpu.make_async_copy(some, some, ag_recv).wait()

    @pl.when(turn >= 27)
    def _():
        some = agb.at[pl.ds(0, 27)]
        pltpu.make_async_copy(some, some, ag_recv).wait()

    kg_ref[...] = agb[...].astype(F32)

    for copy in sent:
        copy.wait_send()

    @pl.when(slab < ns - 1)
    def _():
        up_halo.wait_send()
        up_delta.wait_send()

    @pl.when(slab > 0)
    def _():
        down_halo.wait_send()
        down_delta.wait_send()

    @pl.when(turn < 27)
    def _():
        some = agb.at[pl.ds(0, 26)]
        pltpu.make_async_copy(some, some, rs_send).wait()
        pltpu.make_async_copy(others, others, ag_send).wait()

    @pl.when(turn >= 27)
    def _():
        some = agb.at[pl.ds(0, 27)]
        pltpu.make_async_copy(some, some, rs_send).wait()

    pair_copy.wait_send()
    pltpu.make_async_copy(igr, igr, ig_send).wait()


def write_out(act, ig, kg, act_hbm, ig_hbm, kg_hbm, sem):
    copies = [
        pltpu.make_async_copy(act, act_hbm, sem.at[0]),
        pltpu.make_async_copy(ig, ig_hbm, sem.at[1]),
        pltpu.make_async_copy(kg, kg_hbm, sem.at[2]),
    ]
    for copy in copies:
        copy.start()
    for copy in copies:
        copy.wait()


def device_call(grid, features, kernel, upstream):
    nyl, nxc, nyh, nz = grid
    ns = nyh * nz
    chips = nyl * nxc
    nchan = 2 * chips
    chans = nchan * CB
    shapes = (((FB, 2, 8, NX), BF16), ((CB * 16, NX), F32), ((27, FB, chans), F32))
    features, kernel, upstream = (
        pltpu.with_memory_space_constraint(v, pltpu.HBM) for v in (features, kernel, upstream)
    )
    out = pl.pallas_call(
        functools.partial(body, grid),
        out_shape=tuple(pltpu.VMEM(*s) for s in shapes),
        in_specs=[pl.BlockSpec(memory_space=pltpu.HBM)] * 3,
        out_specs=[pl.BlockSpec(memory_space=pltpu.VMEM)] * 3,
        scratch_shapes=[
            pltpu.VMEM((CB, 2, 8, NX), BF16),
            pltpu.VMEM((27, FB, chans), BF16),
            pltpu.VMEM((FB, 2, 8, NX), BF16),
            pltpu.VMEM((CB * 16, NX), F32),
            pltpu.VMEM((FB * 16, NX), F32),
            pltpu.VMEM((nchan, 2, 8, 16, NX), BF16),
            pltpu.VMEM((4, 8, chans, NX), BF16),
            pltpu.VMEM((2, 2, 12 * FB, 2 * NX), F32),
            pltpu.VMEM((3, 12 * FB, 2 * chans), BF16),
            pltpu.VMEM((chans, 512), BF16),
            pltpu.VMEM((2, 8, FB, NX), BF16),
            pltpu.VMEM((2, 8, FB, NX), BF16),
            pltpu.VMEM((4, 10, 3 * FB, NX), BF16),
            pltpu.VMEM((27, FB, chans), BF16),
            pltpu.VMEM((ns, FB, chans), BF16),
            pltpu.VMEM((27, FB, chans), BF16),
            pltpu.VMEM((2, chips, 8, 16, NX), F32),
            pltpu.VMEM((chips, 8, 16, NX), F32),
            pltpu.VMEM((chips, 8, 16, NX), BF16),
            pltpu.VMEM((chips - 1, 8, 16, NX), BF16),
            pltpu.SemaphoreType.REGULAR((2,)),
            pltpu.SemaphoreType.REGULAR,
            pltpu.SemaphoreType.DMA((3,)),
            pltpu.SemaphoreType.DMA((2, chips)),
            pltpu.SemaphoreType.DMA((2, nchan)),
            pltpu.SemaphoreType.DMA((2, chips)),
            pltpu.SemaphoreType.DMA((2,)),
            pltpu.SemaphoreType.DMA((2,)),
            pltpu.SemaphoreType.DMA((2,)),
            pltpu.SemaphoreType.DMA((2,)),
            pltpu.SemaphoreType.DMA,
            pltpu.SemaphoreType.DMA,
            pltpu.SemaphoreType.DMA,
            pltpu.SemaphoreType.DMA,
            pltpu.SemaphoreType.DMA,
            pltpu.SemaphoreType.DMA,
            pltpu.SemaphoreType.DMA((2,)),
        ],
        compiler_params=pltpu.CompilerParams(
            collective_id=0, has_side_effects=True, vmem_limit_bytes=32 * 1024 * 1024
        ),
    )(features, kernel, upstream)
    out = pl.pallas_call(
        write_out,
        out_shape=tuple(pltpu.HBM(*s) for s in shapes),
        in_specs=[pl.BlockSpec(memory_space=pltpu.VMEM)] * 3,
        out_specs=[pl.BlockSpec(memory_space=pltpu.HBM)] * 3,
        scratch_shapes=[pltpu.SemaphoreType.DMA((3,))],
        compiler_params=pltpu.CompilerParams(vmem_limit_bytes=1024 * 1024),
    )(*out)
    return out[0], out[1].reshape(CB, 2, 8, NX), out[2]


def solution(mesh):
    ns = mesh.shape["slab"]
    specs = (P("chan", "slab", None, None), P(None, "chan", None), P("chan", "slab", None, None))
    out_specs = (
        P("chan", "slab", None, None),
        P("chan", "slab", None, None),
        P(None, "chan", None),
    )
    call = functools.partial(device_call, (2, 4, 2, ns // 2))
    return jax.shard_map(call, mesh=mesh, in_specs=specs, out_specs=out_specs, check_vma=False)
```

```python
import functools

import jax
import jax.numpy as jnp
from jax import lax
from jax.experimental import pallas as pl
from jax.experimental.pallas import tpu as pltpu
from jax.sharding import PartitionSpec as P

MESH = pl.DeviceIdType.MESH
F32 = jnp.float32
BF16 = jnp.bfloat16
CB = 8
FB = 16
NX = 128


def dot(a, b):
    return lax.dot_general(a, b, (((1,), (0,)), ((), ())), preferred_element_type=F32)


def dot_nt(a, b):
    return lax.dot_general(a, b, (((1,), (1,)), ((), ())), preferred_element_type=F32)


def shifted(v, lane):
    left = jnp.where(lane == NX - 1, 0.0, pltpu.roll(v, NX - 1, 1))
    right = jnp.where(lane == 0, 0.0, pltpu.roll(v, 1, 1))
    return left, right


def body(
    grid,
    feat_hbm, kern_hbm, up_hbm,
    act_ref, ig_ref, kg_ref,
    feat, kern, up, rows_f, rows_u, land, xc, tacc, w4, wt, d1, dh, d3, kgs, rsb, agb, igf, igx, igs, igr,
    ring_sem, other_sem, in_sem, g_send, g_recv, f_send, h_send, h_recv, dh_send, dh_recv, rs_send, rs_recv, ag_send, ag_recv, ig_send, ig_recv, pair_sem,
):
    nyl, nxc, nyh, nz = grid
    ns = nyh * nz
    chips = nyl * nxc
    nchan = 2 * chips
    chans = nchan * CB
    reach = nz // 8
    me = lax.axis_index("chan")
    slab = lax.axis_index("slab")
    sz = lax.rem(slab, nz)
    sy = slab // nz
    core = lax.rem(me, 2)
    chip = me // 2
    cx = lax.rem(chip, nxc)
    cy = chip // nxc
    sib = chip * 2 + (1 - core)

    loads = [
        pltpu.make_async_copy(feat_hbm, feat, in_sem.at[0]),
        pltpu.make_async_copy(kern_hbm, kern, in_sem.at[1]),
        pltpu.make_async_copy(up_hbm, up, in_sem.at[2]),
    ]
    for load in loads:
        load.start()

    barrier = pltpu.get_barrier_semaphore()

    def slab_at(dy, dz):
        return lax.rem(sy + dy, nyh) * nz + lax.rem(sz + dz + nz, nz)

    first = nz * 9 // 16
    turn = lax.rem(sz + nz - first, nz) * nyh + sy
    middle = 2 * nyh + 9
    ways = sorted(range(27), key=lambda p: -abs(p - middle))
    tap = sum(jnp.where(turn == p, n, 0) for n, p in enumerate(ways))

    def owner_of(t):
        place = ways[t]
        return (place % nyh) * nz + (place // nyh + first) % nz

    def signal(semaphore, chan, target):
        pl.semaphore_signal(semaphore, inc=1, device_id=(chan, target), device_id_type=MESH)

    hops = [(j, k) for j in range(nyl) for k in range(nxc)][1:]
    hops.sort(key=lambda t: -t[0] - min(t[1], nxc - t[1]))

    def peer(j, k):
        return (lax.rem(cy + j, nyl) * nxc + lax.rem(cx + k, nxc)) * 2 + core

    near = [(0, d) for k in range(1, reach + 1) for d in (k, -k)] + [(1, 0)]
    for dy, dz in reversed(near):
        signal(barrier, me, slab_at(dy, dz))
    for j, k in hops:
        for c in (core, 1 - core):
            signal(barrier, peer(j, k) + c - core, slab)
    signal(barrier, sib, slab)

    @pl.when(slab == nz - 1)
    def _():
        signal(barrier, me, slab + 1)

    @pl.when(slab == nz)
    def _():
        signal(barrier, me, slab - 1)

    loads[0].wait()
    rows_f[...] = feat[...].astype(F32).reshape(CB * 16, NX)
    for z in range(2):
        for yp in range(4):
            pair = [rows_f[pl.ds(z * 8 + 2 * yp + k, CB, stride=16), :] for k in range(2)]
            land[me, 0, z * 4 + yp] = jnp.concatenate(pair, 0).astype(BF16)

    pl.semaphore_wait(barrier, nchan - 1 + len(near) + jnp.where((slab == nz - 1) | (slab == nz), 1, 0))

    def tell(n):
        for d in (reach << n, -(reach << n)):
            signal(ring_sem.at[n], me, slab_at(0, d))

    tell(0)

    up_halo = pltpu.make_async_remote_copy(
        src_ref=land.at[me, 0, pl.ds(4, 4)], dst_ref=land.at[me, 1, pl.ds(0, 4)],
        send_sem=h_send.at[0], recv_sem=h_recv.at[0], device_id=(me, slab + 1), device_id_type=MESH)
    down_halo = pltpu.make_async_remote_copy(
        src_ref=land.at[me, 0, pl.ds(0, 4)], dst_ref=land.at[me, 1, pl.ds(4, 4)],
        send_sem=h_send.at[1], recv_sem=h_recv.at[1], device_id=(me, slab - 1), device_id_type=MESH)

    @pl.when(slab < ns - 1)
    def _():
        up_halo.start()

    @pl.when(slab > 0)
    def _():
        down_halo.start()

    def source(j, k):
        return (lax.rem(cy + nyl - j, nyl) * nxc + lax.rem(cx + nxc - k, nxc)) * 2 + core

    def gather_copy(part, holder, target, send_sem):
        return pltpu.make_async_remote_copy(
            src_ref=land.at[holder, part], dst_ref=land.at[holder, part],
            send_sem=send_sem, recv_sem=g_recv.at[part, holder], device_id=(target, slab), device_id_type=MESH)

    sent = []

    def send_own(part):
        for n, (j, k) in enumerate(hops):
            copy = gather_copy(part, me, peer(j, k), g_send.at[part, n])
            copy.start()
            sent.append(copy)
        copy = gather_copy(part, me, sib, g_send.at[part, chips - 1])
        copy.start()
        sent.append(copy)

    def forward(part):
        for n, (j, k) in enumerate(hops):
            holder = source(j, k)
            copy = gather_copy(part, holder, sib, f_send.at[part, n])
            copy.wait_recv()
            copy.start()
            sent.append(copy)

    def receive_rest(part):
        for q in range(chips):
            holder = lax.rem(chip + q, chips) * 2 + (1 - core)
            gather_copy(part, holder, sib, f_send.at[part, 0]).wait_recv()

    send_own(0)

    loads[1].wait()
    for a in range(3):
        taps = [kern[pl.ds(9 * a + 3 * b, 3)].reshape(3 * FB, chans) for b in range(3)]
        zero = jnp.zeros((3 * FB, chans), BF16)
        w4[a] = jnp.concatenate(
            [
                jnp.concatenate([taps[2], zero], 1),
                jnp.concatenate([taps[1], taps[2]], 1),
                jnp.concatenate([taps[0], taps[1]], 1),
                jnp.concatenate([zero, taps[0]], 1),
            ],
            0,
        )
    d3[...] = jnp.zeros(d3.shape, BF16)

    @pl.when(slab == 0)
    def _():
        land[me, 1, pl.ds(0, 4)] = jnp.zeros((4, 16, NX), BF16)

    @pl.when(slab == ns - 1)
    def _():
        land[me, 1, pl.ds(4, 4)] = jnp.zeros((4, 16, NX), BF16)

    @pl.when(slab > 0)
    def _():
        up_halo.wait_recv()

    @pl.when(slab < ns - 1)
    def _():
        down_halo.wait_recv()

    send_own(1)
    pl.semaphore_wait(ring_sem.at[0], 2)
    tell(1)

    flipped = [kern[9 * a + 3 * b + e].astype(F32) for a in (2, 1, 0) for b in (2, 1, 0) for e in range(3)]
    flipped += [jnp.zeros((FB, chans), F32)] * 5
    for q in range(4):
        wt[:, pl.ds(q * 128, 128)] = jnp.transpose(jnp.concatenate(flipped[8 * q : 8 * q + 8], 0)).astype(BF16)

    loads[2].wait()
    rows_u[...] = up[...].astype(F32).reshape(FB * 16, NX)

    def unpack(part):
        for zi in range(2):
            z = (1, 2)[zi] if part == 0 else (0, 3)[zi]
            for yp in range(4):
                tiles = land[:, part, zi * 4 + yp].astype(F32)
                for k in range(2):
                    xc[z, 2 * yp + k] = tiles[:, CB * k : CB * k + CB].reshape(chans, NX).astype(BF16)

    def pair_rows(z, yp):
        return xc[z, pl.ds(2 * yp, 2)].reshape(2 * chans, NX)

    forward(0)
    pl.semaphore_wait(ring_sem.at[1], 2)
    signal(other_sem, me, slab_at(1, 0))
    receive_rest(0)
    unpack(0)
    for o in range(2):
        weights = jnp.concatenate([w4[1 - o], w4[2 - o]], 1)
        for q in range(2):
            cells = jnp.concatenate(
                [jnp.concatenate([pair_rows(z, 2 * q + k) for z in (1, 2)], 0) for k in range(2)], 1)
            tacc[o, q] = dot(weights, cells)

    forward(1)
    receive_rest(1)
    unpack(1)
    for o in range(2):
        for q in range(2):
            cells = jnp.concatenate([pair_rows(3 * o, 2 * q + k) for k in range(2)], 1)
            tacc[o, q] += dot(w4[2 * o], cells)

    lane = lax.broadcasted_iota(jnp.int32, (FB, NX), 1)

    def pair_sum(o, yp, yo):
        return tacc[o, yp // 2, pl.ds(yo * 3 * FB, 3 * FB), pl.ds((yp % 2) * NX, NX)]

    acts = []
    for o in range(2):
        for y in range(8):
            yp, r = y // 2, y % 2
            total = pair_sum(o, yp, 1 + r)
            if r == 0 and yp > 0:
                total = total + pair_sum(o, yp - 1, 3)
            if r == 1 and yp < 3:
                total = total + pair_sum(o, yp + 1, 0)
            from_left = shifted(total[0:FB], lane)[1]
            from_right = shifted(total[2 * FB : 3 * FB], lane)[0]
            pre = total[FB : 2 * FB] + from_left + from_right
            s = 1.0 / (1.0 + jnp.exp(-jnp.maximum(pre, -88.0)))
            upstream = rows_u[pl.ds(o * 8 + y, FB, stride=16), :]
            delta = (upstream * s * (1.0 + pre * (1.0 - s))).astype(BF16)
            rows_u[pl.ds(o * 8 + y, FB, stride=16), :] = pre * s
            d1[o, y] = delta
            left, right = shifted(delta.astype(F32), lane)
            d3[1 + o, 1 + y] = jnp.concatenate([left.astype(BF16), delta, right.astype(BF16)], 0)

    up_delta = pltpu.make_async_remote_copy(
        src_ref=d1.at[1], dst_ref=dh.at[0],
        send_sem=dh_send.at[0], recv_sem=dh_recv.at[0], device_id=(me, slab + 1), device_id_type=MESH)
    down_delta = pltpu.make_async_remote_copy(
        src_ref=d1.at[0], dst_ref=dh.at[1],
        send_sem=dh_send.at[1], recv_sem=dh_recv.at[1], device_id=(me, slab - 1), device_id_type=MESH)

    @pl.when(slab < ns - 1)
    def _():
        up_delta.start()

    @pl.when(slab > 0)
    def _():
        down_delta.start()

    for a in range(3):
        lhs = jnp.concatenate(
            [d3[1 + o, pl.ds(2 * yp, 4)].reshape(12 * FB, NX) for o in range(2) for yp in range(4)], 1)
        rhs = jnp.concatenate([pair_rows(o + a, yp) for o in range(2) for yp in range(4)], 1)
        g = dot_nt(lhs, rhs)
        for b in range(3):
            term = (
                g[(2 - b) * 3 * FB : (3 - b) * 3 * FB, :chans] + g[(3 - b) * 3 * FB : (4 - b) * 3 * FB, chans:]
            )
            kgs[pl.ds(9 * a + 3 * b, 3)] = term.reshape(3, FB, chans).astype(BF16)
        if a == 0:
            pl.semaphore_wait(other_sem, 1)
        for t in range(9 * a, 9 * a + 9):
            send = pltpu.make_async_remote_copy(
                src_ref=kgs.at[t], dst_ref=rsb.at[slab],
                send_sem=rs_send, recv_sem=rs_recv, device_id=(me, owner_of(t)), device_id_type=MESH)

            @pl.when(slab != owner_of(t))
            def _():
                send.start()

    act_ref[...] = rows_u[...].reshape(FB, 2, 8, NX).astype(BF16)

    def place_halo(plane, z):
        for y in range(8):
            delta = dh[plane, y]
            left, right = shifted(delta.astype(F32), lane)
            d3[z, 1 + y] = jnp.concatenate([left.astype(BF16), delta, right.astype(BF16)], 0)

    @pl.when(slab > 0)
    def _():
        up_delta.wait_recv()
        place_halo(0, 0)

    @pl.when(slab < ns - 1)
    def _():
        down_delta.wait_recv()
        place_halo(1, 3)

    blank = jnp.zeros((80, 2 * NX), BF16)
    for o in range(2):
        for yp in range(4):
            cells = jnp.concatenate(
                [
                    jnp.concatenate(
                        [d3[o + z, pl.ds(2 * yp + k, 3)].reshape(9 * FB, NX) for z in range(3)], 0)
                    for k in range(2)
                ],
                1,
            )
            grad = dot(wt[...], jnp.concatenate([cells, blank], 0)).reshape(chips, 2, CB, 2 * NX)
            grad = jnp.concatenate([grad[..., :NX], grad[..., NX:]], 2)
            for c in range(2):
                igf[c, :, o * 4 + yp] = grad[:, c]

    pair_copy = pltpu.make_async_remote_copy(
        src_ref=igf.at[1 - core], dst_ref=igx,
        send_sem=pair_sem.at[0], recv_sem=pair_sem.at[1], device_id=(sib, slab), device_id_type=MESH)
    pair_copy.start()
    pair_copy.wait_recv()
    for q in range(chips):
        igs[q] = (igf[core, q] + igx[q]).astype(BF16)
    for n, (j, k) in enumerate(hops):
        target = peer(j, k)
        pltpu.make_async_remote_copy(
            src_ref=igs.at[target // 2], dst_ref=igr.at[n],
            send_sem=ig_send, recv_sem=ig_recv, device_id=(target, slab), device_id_type=MESH).start()

    others = rsb.at[pl.ds(0, ns - 1)]

    @pl.when(turn < 27)
    def _():
        rsb[slab] = kgs[tap]
        pltpu.make_async_copy(others, others, rs_recv).wait()
        total = rsb[0].astype(F32)
        for k in range(1, ns):
            total = total + rsb[k].astype(F32)
        agb[tap] = total.astype(BF16)
        for target in sorted(range(ns), key=lambda t: min(t % nz, nz - t % nz)):
            share = pltpu.make_async_remote_copy(
                src_ref=agb.at[tap], dst_ref=agb.at[tap],
                send_sem=ag_send, recv_sem=ag_recv, device_id=(me, target), device_id_type=MESH)

            @pl.when(slab != target)
            def _():
                share.start()

    pltpu.make_async_copy(igr, igr, ig_recv).wait()
    for q in range(8):
        total = igs[chip, q].astype(F32)
        for k in range(chips - 1):
            total = total + igr[k, q].astype(F32)
        for k in range(2):
            ig_ref[pl.ds((q // 4) * 8 + 2 * (q % 4) + k, CB, stride=16), :] = total[CB * k : CB * k + CB]

    for copy in sent:
        copy.wait_send()

    @pl.when(slab < ns - 1)
    def _():
        up_halo.wait_send()
        up_delta.wait_send()

    @pl.when(slab > 0)
    def _():
        down_halo.wait_send()
        down_delta.wait_send()

    @pl.when(turn < 27)
    def _():
        some = agb.at[pl.ds(0, 26)]
        pltpu.make_async_copy(some, some, rs_send).wait()

    @pl.when(turn >= 27)
    def _():
        some = agb.at[pl.ds(0, 27)]
        pltpu.make_async_copy(some, some, rs_send).wait()

    pair_copy.wait_send()
    pltpu.make_async_copy(igr, igr, ig_send).wait()

    @pl.when(turn < 27)
    def _():
        some = agb.at[pl.ds(0, 26)]
        pltpu.make_async_copy(some, some, ag_recv).wait()

    @pl.when(turn >= 27)
    def _():
        some = agb.at[pl.ds(0, 27)]
        pltpu.make_async_copy(some, some, ag_recv).wait()

    kg_ref[...] = agb[...].astype(F32)

    @pl.when(turn < 27)
    def _():
        pltpu.make_async_copy(others, others, ag_send).wait()


def write_out(act, ig, kg, act_hbm, ig_hbm, kg_hbm, sem):
    copies = [
        pltpu.make_async_copy(act, act_hbm, sem.at[0]),
        pltpu.make_async_copy(ig, ig_hbm, sem.at[1]),
        pltpu.make_async_copy(kg, kg_hbm, sem.at[2]),
    ]
    for copy in copies:
        copy.start()
    for copy in copies:
        copy.wait()


def device_call(grid, features, kernel, upstream):
    nyl, nxc, nyh, nz = grid
    ns = nyh * nz
    chips = nyl * nxc
    nchan = 2 * chips
    chans = nchan * CB
    shapes = (((FB, 2, 8, NX), BF16), ((CB * 16, NX), F32), ((27, FB, chans), F32))
    features, kernel, upstream = (
        pltpu.with_memory_space_constraint(v, pltpu.HBM) for v in (features, kernel, upstream)
    )
    out = pl.pallas_call(
        functools.partial(body, grid),
        out_shape=tuple(pltpu.VMEM(*s) for s in shapes),
        in_specs=[pl.BlockSpec(memory_space=pltpu.HBM)] * 3,
        out_specs=[pl.BlockSpec(memory_space=pltpu.VMEM)] * 3,
        scratch_shapes=[
            pltpu.VMEM((CB, 2, 8, NX), BF16),
            pltpu.VMEM((27, FB, chans), BF16),
            pltpu.VMEM((FB, 2, 8, NX), BF16),
            pltpu.VMEM((CB * 16, NX), F32),
            pltpu.VMEM((FB * 16, NX), F32),
            pltpu.VMEM((nchan, 2, 8, 16, NX), BF16),
            pltpu.VMEM((4, 8, chans, NX), BF16),
            pltpu.VMEM((2, 2, 12 * FB, 2 * NX), F32),
            pltpu.VMEM((3, 12 * FB, 2 * chans), BF16),
            pltpu.VMEM((chans, 512), BF16),
            pltpu.VMEM((2, 8, FB, NX), BF16),
            pltpu.VMEM((2, 8, FB, NX), BF16),
            pltpu.VMEM((4, 10, 3 * FB, NX), BF16),
            pltpu.VMEM((27, FB, chans), BF16),
            pltpu.VMEM((ns, FB, chans), BF16),
            pltpu.VMEM((27, FB, chans), BF16),
            pltpu.VMEM((2, chips, 8, 16, NX), F32),
            pltpu.VMEM((chips, 8, 16, NX), F32),
            pltpu.VMEM((chips, 8, 16, NX), BF16),
            pltpu.VMEM((chips - 1, 8, 16, NX), BF16),
            pltpu.SemaphoreType.REGULAR((2,)),
            pltpu.SemaphoreType.REGULAR,
            pltpu.SemaphoreType.DMA((3,)),
            pltpu.SemaphoreType.DMA((2, chips)),
            pltpu.SemaphoreType.DMA((2, nchan)),
            pltpu.SemaphoreType.DMA((2, chips)),
            pltpu.SemaphoreType.DMA((2,)),
            pltpu.SemaphoreType.DMA((2,)),
            pltpu.SemaphoreType.DMA((2,)),
            pltpu.SemaphoreType.DMA((2,)),
            pltpu.SemaphoreType.DMA,
            pltpu.SemaphoreType.DMA,
            pltpu.SemaphoreType.DMA,
            pltpu.SemaphoreType.DMA,
            pltpu.SemaphoreType.DMA,
            pltpu.SemaphoreType.DMA,
            pltpu.SemaphoreType.DMA((2,)),
        ],
        compiler_params=pltpu.CompilerParams(
            collective_id=0, has_side_effects=True, vmem_limit_bytes=32 * 1024 * 1024
        ),
    )(features, kernel, upstream)
    out = pl.pallas_call(
        write_out,
        out_shape=tuple(pltpu.HBM(*s) for s in shapes),
        in_specs=[pl.BlockSpec(memory_space=pltpu.VMEM)] * 3,
        out_specs=[pl.BlockSpec(memory_space=pltpu.HBM)] * 3,
        scratch_shapes=[pltpu.SemaphoreType.DMA((3,))],
        compiler_params=pltpu.CompilerParams(vmem_limit_bytes=1024 * 1024),
    )(*out)
    return out[0], out[1].reshape(CB, 2, 8, NX), out[2]


def solution(mesh):
    ns = mesh.shape["slab"]
    specs = (P("chan", "slab", None, None), P(None, "chan", None), P("chan", "slab", None, None))
    out_specs = (
        P("chan", "slab", None, None),
        P("chan", "slab", None, None),
        P(None, "chan", None),
    )
    call = functools.partial(device_call, (2, 4, 2, ns // 2))
    return jax.shard_map(call, mesh=mesh, in_specs=specs, out_specs=out_specs, check_vma=False)
```

```python
import functools

import jax
import jax.numpy as jnp
from jax import lax
from jax.experimental import pallas as pl
from jax.experimental.pallas import tpu as pltpu
from jax.sharding import PartitionSpec as P

MESH = pl.DeviceIdType.MESH
F32 = jnp.float32
BF16 = jnp.bfloat16
CB = 8
FB = 16
NX = 128


def dot(a, b):
    return lax.dot_general(a, b, (((1,), (0,)), ((), ())), preferred_element_type=F32)


def dot_nt(a, b):
    return lax.dot_general(a, b, (((1,), (1,)), ((), ())), preferred_element_type=F32)


def shifted(v, lane):
    left = jnp.where(lane == NX - 1, 0.0, pltpu.roll(v, NX - 1, 1))
    right = jnp.where(lane == 0, 0.0, pltpu.roll(v, 1, 1))
    return left, right


def body(
    grid,
    feat_hbm, kern_hbm, up_hbm,
    act_ref, ig_ref, kg_ref,
    feat, kern, up, rows_f, rows_u, land, xc, tacc, w4, wt, d1, dh, d3, kgs, rsb, agb, igf, igx, igs, igr,
    ring_sem, other_sem, in_sem, g_send, g_recv, f_send, h_send, h_recv, dh_send, dh_recv, rs_send, rs_recv, ag_send, ag_recv, ig_send, ig_recv, pair_sem,
):
    nyl, nxc, nyh, nz = grid
    ns = nyh * nz
    chips = nyl * nxc
    nchan = 2 * chips
    chans = nchan * CB
    reach = nz // 8
    me = lax.axis_index("chan")
    slab = lax.axis_index("slab")
    sz = lax.rem(slab, nz)
    sy = slab // nz
    core = lax.rem(me, 2)
    chip = me // 2
    cx = lax.rem(chip, nxc)
    cy = chip // nxc
    sib = chip * 2 + (1 - core)

    loads = [
        pltpu.make_async_copy(feat_hbm, feat, in_sem.at[0]),
        pltpu.make_async_copy(kern_hbm, kern, in_sem.at[1]),
        pltpu.make_async_copy(up_hbm, up, in_sem.at[2]),
    ]
    for load in loads:
        load.start()

    barrier = pltpu.get_barrier_semaphore()

    def slab_at(dy, dz):
        return lax.rem(sy + dy, nyh) * nz + lax.rem(sz + dz + nz, nz)

    first = nz * 9 // 16
    turn = lax.rem(sz + nz - first, nz) * nyh + sy
    middle = 2 * nyh + 9
    ways = sorted(range(27), key=lambda p: -abs(p - middle))
    tap = sum(jnp.where(turn == p, n, 0) for n, p in enumerate(ways))

    def owner_of(t):
        place = ways[t]
        return (place % nyh) * nz + (place // nyh + first) % nz

    def signal(semaphore, chan, target):
        pl.semaphore_signal(semaphore, inc=1, device_id=(chan, target), device_id_type=MESH)

    hops = [(j, k) for j in range(nyl) for k in range(nxc)][1:]
    hops.sort(key=lambda t: -t[0] - min(t[1], nxc - t[1]))

    def peer(j, k):
        return (lax.rem(cy + j, nyl) * nxc + lax.rem(cx + k, nxc)) * 2 + core

    near = [(0, d) for k in range(1, reach + 1) for d in (k, -k)] + [(1, 0)]
    for dy, dz in reversed(near):
        signal(barrier, me, slab_at(dy, dz))
    for j, k in hops:
        for c in (core, 1 - core):
            signal(barrier, peer(j, k) + c - core, slab)
    signal(barrier, sib, slab)

    @pl.when(slab == nz - 1)
    def _():
        signal(barrier, me, slab + 1)

    @pl.when(slab == nz)
    def _():
        signal(barrier, me, slab - 1)

    loads[0].wait()
    rows_f[...] = feat[...].astype(F32).reshape(CB * 16, NX)
    for z in range(2):
        for yp in range(4):
            pair = [rows_f[pl.ds(z * 8 + 2 * yp + k, CB, stride=16), :] for k in range(2)]
            land[me, 0, z * 4 + yp] = jnp.concatenate(pair, 0).astype(BF16)

    pl.semaphore_wait(barrier, nchan - 1 + len(near) + jnp.where((slab == nz - 1) | (slab == nz), 1, 0))

    def tell(n):
        for d in (reach << n, -(reach << n)):
            signal(ring_sem.at[n], me, slab_at(0, d))

    tell(0)

    up_halo = pltpu.make_async_remote_copy(
        src_ref=land.at[me, 0, pl.ds(4, 4)], dst_ref=land.at[me, 1, pl.ds(0, 4)],
        send_sem=h_send.at[0], recv_sem=h_recv.at[0], device_id=(me, slab + 1), device_id_type=MESH)
    down_halo = pltpu.make_async_remote_copy(
        src_ref=land.at[me, 0, pl.ds(0, 4)], dst_ref=land.at[me, 1, pl.ds(4, 4)],
        send_sem=h_send.at[1], recv_sem=h_recv.at[1], device_id=(me, slab - 1), device_id_type=MESH)

    @pl.when(slab < ns - 1)
    def _():
        up_halo.start()

    @pl.when(slab > 0)
    def _():
        down_halo.start()

    def source(j, k):
        return (lax.rem(cy + nyl - j, nyl) * nxc + lax.rem(cx + nxc - k, nxc)) * 2 + core

    def gather_copy(part, holder, target, send_sem):
        return pltpu.make_async_remote_copy(
            src_ref=land.at[holder, part], dst_ref=land.at[holder, part],
            send_sem=send_sem, recv_sem=g_recv.at[part, holder], device_id=(target, slab), device_id_type=MESH)

    sent = []

    def send_own(part):
        copy = gather_copy(part, me, sib, g_send.at[part, chips - 1])
        copy.start()
        sent.append(copy)
        for n, (j, k) in enumerate(hops):
            copy = gather_copy(part, me, peer(j, k), g_send.at[part, n])
            copy.start()
            sent.append(copy)

    def forward(part):
        for n, (j, k) in enumerate(hops):
            holder = source(j, k)
            copy = gather_copy(part, holder, sib, f_send.at[part, n])
            copy.wait_recv()
            copy.start()
            sent.append(copy)

    def receive_rest(part):
        for q in range(chips):
            holder = lax.rem(chip + q, chips) * 2 + (1 - core)
            gather_copy(part, holder, sib, f_send.at[part, 0]).wait_recv()

    send_own(0)

    loads[1].wait()
    for a in range(3):
        taps = [kern[pl.ds(9 * a + 3 * b, 3)].reshape(3 * FB, chans) for b in range(3)]
        zero = jnp.zeros((3 * FB, chans), BF16)
        w4[a] = jnp.concatenate(
            [
                jnp.concatenate([taps[2], zero], 1),
                jnp.concatenate([taps[1], taps[2]], 1),
                jnp.concatenate([taps[0], taps[1]], 1),
                jnp.concatenate([zero, taps[0]], 1),
            ],
            0,
        )
    d3[...] = jnp.zeros(d3.shape, BF16)

    @pl.when(slab == 0)
    def _():
        land[me, 1, pl.ds(0, 4)] = jnp.zeros((4, 16, NX), BF16)

    @pl.when(slab == ns - 1)
    def _():
        land[me, 1, pl.ds(4, 4)] = jnp.zeros((4, 16, NX), BF16)

    @pl.when(slab > 0)
    def _():
        up_halo.wait_recv()

    @pl.when(slab < ns - 1)
    def _():
        down_halo.wait_recv()

    send_own(1)
    pl.semaphore_wait(ring_sem.at[0], 2)
    tell(1)

    flipped = [kern[9 * a + 3 * b + e].astype(F32) for a in (2, 1, 0) for b in (2, 1, 0) for e in range(3)]
    flipped += [jnp.zeros((FB, chans), F32)] * 5
    for q in range(4):
        wt[:, pl.ds(q * 128, 128)] = jnp.transpose(jnp.concatenate(flipped[8 * q : 8 * q + 8], 0)).astype(BF16)

    loads[2].wait()
    rows_u[...] = up[...].astype(F32).reshape(FB * 16, NX)

    def unpack(part):
        for zi in range(2):
            z = (1, 2)[zi] if part == 0 else (0, 3)[zi]
            for yp in range(4):
                tiles = land[:, part, zi * 4 + yp].astype(F32)
                for k in range(2):
                    xc[z, 2 * yp + k] = tiles[:, CB * k : CB * k + CB].reshape(chans, NX).astype(BF16)

    def pair_rows(z, yp):
        return xc[z, pl.ds(2 * yp, 2)].reshape(2 * chans, NX)

    forward(0)
    pl.semaphore_wait(ring_sem.at[1], 2)
    signal(other_sem, me, slab_at(1, 0))
    receive_rest(0)
    unpack(0)
    for o in range(2):
        weights = jnp.concatenate([w4[1 - o], w4[2 - o]], 1)
        for q in range(2):
            cells = jnp.concatenate(
                [jnp.concatenate([pair_rows(z, 2 * q + k) for z in (1, 2)], 0) for k in range(2)], 1)
            tacc[o, q] = dot(weights, cells)

    forward(1)
    receive_rest(1)
    unpack(1)
    for o in range(2):
        for q in range(2):
            cells = jnp.concatenate([pair_rows(3 * o, 2 * q + k) for k in range(2)], 1)
            tacc[o, q] += dot(w4[2 * o], cells)

    lane = lax.broadcasted_iota(jnp.int32, (FB, NX), 1)

    def pair_sum(o, yp, yo):
        return tacc[o, yp // 2, pl.ds(yo * 3 * FB, 3 * FB), pl.ds((yp % 2) * NX, NX)]

    acts = []
    for o in range(2):
        for y in range(8):
            yp, r = y // 2, y % 2
            total = pair_sum(o, yp, 1 + r)
            if r == 0 and yp > 0:
                total = total + pair_sum(o, yp - 1, 3)
            if r == 1 and yp < 3:
                total = total + pair_sum(o, yp + 1, 0)
            from_left = shifted(total[0:FB], lane)[1]
            from_right = shifted(total[2 * FB : 3 * FB], lane)[0]
            pre = total[FB : 2 * FB] + from_left + from_right
            s = 1.0 / (1.0 + jnp.exp(-jnp.maximum(pre, -88.0)))
            upstream = rows_u[pl.ds(o * 8 + y, FB, stride=16), :]
            delta = (upstream * s * (1.0 + pre * (1.0 - s))).astype(BF16)
            rows_u[pl.ds(o * 8 + y, FB, stride=16), :] = pre * s
            d1[o, y] = delta
            left, right = shifted(delta.astype(F32), lane)
            d3[1 + o, 1 + y] = jnp.concatenate([left.astype(BF16), delta, right.astype(BF16)], 0)

    up_delta = pltpu.make_async_remote_copy(
        src_ref=d1.at[1], dst_ref=dh.at[0],
        send_sem=dh_send.at[0], recv_sem=dh_recv.at[0], device_id=(me, slab + 1), device_id_type=MESH)
    down_delta = pltpu.make_async_remote_copy(
        src_ref=d1.at[0], dst_ref=dh.at[1],
        send_sem=dh_send.at[1], recv_sem=dh_recv.at[1], device_id=(me, slab - 1), device_id_type=MESH)

    @pl.when(slab < ns - 1)
    def _():
        up_delta.start()

    @pl.when(slab > 0)
    def _():
        down_delta.start()

    for a in range(3):
        lhs = jnp.concatenate(
            [d3[1 + o, pl.ds(2 * yp, 4)].reshape(12 * FB, NX) for o in range(2) for yp in range(4)], 1)
        rhs = jnp.concatenate([pair_rows(o + a, yp) for o in range(2) for yp in range(4)], 1)
        g = dot_nt(lhs, rhs)
        for b in range(3):
            term = (
                g[(2 - b) * 3 * FB : (3 - b) * 3 * FB, :chans] + g[(3 - b) * 3 * FB : (4 - b) * 3 * FB, chans:]
            )
            kgs[pl.ds(9 * a + 3 * b, 3)] = term.reshape(3, FB, chans).astype(BF16)
        if a == 0:
            pl.semaphore_wait(other_sem, 1)
        for t in range(9 * a, 9 * a + 9):
            send = pltpu.make_async_remote_copy(
                src_ref=kgs.at[t], dst_ref=rsb.at[slab],
                send_sem=rs_send, recv_sem=rs_recv, device_id=(me, owner_of(t)), device_id_type=MESH)

            @pl.when(slab != owner_of(t))
            def _():
                send.start()

    act_ref[...] = rows_u[...].reshape(FB, 2, 8, NX).astype(BF16)

    def place_halo(plane, z):
        for y in range(8):
            delta = dh[plane, y]
            left, right = shifted(delta.astype(F32), lane)
            d3[z, 1 + y] = jnp.concatenate([left.astype(BF16), delta, right.astype(BF16)], 0)

    @pl.when(slab > 0)
    def _():
        up_delta.wait_recv()
        place_halo(0, 0)

    @pl.when(slab < ns - 1)
    def _():
        down_delta.wait_recv()
        place_halo(1, 3)

    blank = jnp.zeros((80, 2 * NX), BF16)
    for o in range(2):
        for yp in range(4):
            cells = jnp.concatenate(
                [
                    jnp.concatenate(
                        [d3[o + z, pl.ds(2 * yp + k, 3)].reshape(9 * FB, NX) for z in range(3)], 0)
                    for k in range(2)
                ],
                1,
            )
            grad = dot(wt[...], jnp.concatenate([cells, blank], 0)).reshape(chips, 2, CB, 2 * NX)
            grad = jnp.concatenate([grad[..., :NX], grad[..., NX:]], 2)
            for c in range(2):
                igf[c, :, o * 4 + yp] = grad[:, c]

    pair_copy = pltpu.make_async_remote_copy(
        src_ref=igf.at[1 - core], dst_ref=igx,
        send_sem=pair_sem.at[0], recv_sem=pair_sem.at[1], device_id=(sib, slab), device_id_type=MESH)
    pair_copy.start()
    pair_copy.wait_recv()
    for q in range(chips):
        igs[q] = (igf[core, q] + igx[q]).astype(BF16)
    for n, (j, k) in enumerate(hops):
        target = peer(j, k)
        pltpu.make_async_remote_copy(
            src_ref=igs.at[target // 2], dst_ref=igr.at[n],
            send_sem=ig_send, recv_sem=ig_recv, device_id=(target, slab), device_id_type=MESH).start()

    others = rsb.at[pl.ds(0, ns - 1)]

    @pl.when(turn < 27)
    def _():
        rsb[slab] = kgs[tap]
        pltpu.make_async_copy(others, others, rs_recv).wait()
        total = rsb[0].astype(F32)
        for k in range(1, ns):
            total = total + rsb[k].astype(F32)
        agb[tap] = total.astype(BF16)
        for target in sorted(range(ns), key=lambda t: min(t % nz, nz - t % nz)):
            share = pltpu.make_async_remote_copy(
                src_ref=agb.at[tap], dst_ref=agb.at[tap],
                send_sem=ag_send, recv_sem=ag_recv, device_id=(me, target), device_id_type=MESH)

            @pl.when(slab != target)
            def _():
                share.start()

    pltpu.make_async_copy(igr, igr, ig_recv).wait()
    for q in range(8):
        total = igs[chip, q].astype(F32)
        for k in range(chips - 1):
            total = total + igr[k, q].astype(F32)
        for k in range(2):
            ig_ref[pl.ds((q // 4) * 8 + 2 * (q % 4) + k, CB, stride=16), :] = total[CB * k : CB * k + CB]

    for copy in sent:
        copy.wait_send()

    @pl.when(slab < ns - 1)
    def _():
        up_halo.wait_send()
        up_delta.wait_send()

    @pl.when(slab > 0)
    def _():
        down_halo.wait_send()
        down_delta.wait_send()

    @pl.when(turn < 27)
    def _():
        some = agb.at[pl.ds(0, 26)]
        pltpu.make_async_copy(some, some, rs_send).wait()

    @pl.when(turn >= 27)
    def _():
        some = agb.at[pl.ds(0, 27)]
        pltpu.make_async_copy(some, some, rs_send).wait()

    pair_copy.wait_send()
    pltpu.make_async_copy(igr, igr, ig_send).wait()

    @pl.when(turn < 27)
    def _():
        some = agb.at[pl.ds(0, 26)]
        pltpu.make_async_copy(some, some, ag_recv).wait()

    @pl.when(turn >= 27)
    def _():
        some = agb.at[pl.ds(0, 27)]
        pltpu.make_async_copy(some, some, ag_recv).wait()

    kg_ref[...] = agb[...].astype(F32)

    @pl.when(turn < 27)
    def _():
        pltpu.make_async_copy(others, others, ag_send).wait()


def write_out(act, ig, kg, act_hbm, ig_hbm, kg_hbm, sem):
    copies = [
        pltpu.make_async_copy(act, act_hbm, sem.at[0]),
        pltpu.make_async_copy(ig, ig_hbm, sem.at[1]),
        pltpu.make_async_copy(kg, kg_hbm, sem.at[2]),
    ]
    for copy in copies:
        copy.start()
    for copy in copies:
        copy.wait()


def device_call(grid, features, kernel, upstream):
    nyl, nxc, nyh, nz = grid
    ns = nyh * nz
    chips = nyl * nxc
    nchan = 2 * chips
    chans = nchan * CB
    shapes = (((FB, 2, 8, NX), BF16), ((CB * 16, NX), F32), ((27, FB, chans), F32))
    features, kernel, upstream = (
        pltpu.with_memory_space_constraint(v, pltpu.HBM) for v in (features, kernel, upstream)
    )
    out = pl.pallas_call(
        functools.partial(body, grid),
        out_shape=tuple(pltpu.VMEM(*s) for s in shapes),
        in_specs=[pl.BlockSpec(memory_space=pltpu.HBM)] * 3,
        out_specs=[pl.BlockSpec(memory_space=pltpu.VMEM)] * 3,
        scratch_shapes=[
            pltpu.VMEM((CB, 2, 8, NX), BF16),
            pltpu.VMEM((27, FB, chans), BF16),
            pltpu.VMEM((FB, 2, 8, NX), BF16),
            pltpu.VMEM((CB * 16, NX), F32),
            pltpu.VMEM((FB * 16, NX), F32),
            pltpu.VMEM((nchan, 2, 8, 16, NX), BF16),
            pltpu.VMEM((4, 8, chans, NX), BF16),
            pltpu.VMEM((2, 2, 12 * FB, 2 * NX), F32),
            pltpu.VMEM((3, 12 * FB, 2 * chans), BF16),
            pltpu.VMEM((chans, 512), BF16),
            pltpu.VMEM((2, 8, FB, NX), BF16),
            pltpu.VMEM((2, 8, FB, NX), BF16),
            pltpu.VMEM((4, 10, 3 * FB, NX), BF16),
            pltpu.VMEM((27, FB, chans), BF16),
            pltpu.VMEM((ns, FB, chans), BF16),
            pltpu.VMEM((27, FB, chans), BF16),
            pltpu.VMEM((2, chips, 8, 16, NX), F32),
            pltpu.VMEM((chips, 8, 16, NX), F32),
            pltpu.VMEM((chips, 8, 16, NX), BF16),
            pltpu.VMEM((chips - 1, 8, 16, NX), BF16),
            pltpu.SemaphoreType.REGULAR((2,)),
            pltpu.SemaphoreType.REGULAR,
            pltpu.SemaphoreType.DMA((3,)),
            pltpu.SemaphoreType.DMA((2, chips)),
            pltpu.SemaphoreType.DMA((2, nchan)),
            pltpu.SemaphoreType.DMA((2, chips)),
            pltpu.SemaphoreType.DMA((2,)),
            pltpu.SemaphoreType.DMA((2,)),
            pltpu.SemaphoreType.DMA((2,)),
            pltpu.SemaphoreType.DMA((2,)),
            pltpu.SemaphoreType.DMA,
            pltpu.SemaphoreType.DMA,
            pltpu.SemaphoreType.DMA,
            pltpu.SemaphoreType.DMA,
            pltpu.SemaphoreType.DMA,
            pltpu.SemaphoreType.DMA,
            pltpu.SemaphoreType.DMA((2,)),
        ],
        compiler_params=pltpu.CompilerParams(
            collective_id=0, has_side_effects=True, vmem_limit_bytes=32 * 1024 * 1024
        ),
    )(features, kernel, upstream)
    out = pl.pallas_call(
        write_out,
        out_shape=tuple(pltpu.HBM(*s) for s in shapes),
        in_specs=[pl.BlockSpec(memory_space=pltpu.VMEM)] * 3,
        out_specs=[pl.BlockSpec(memory_space=pltpu.HBM)] * 3,
        scratch_shapes=[pltpu.SemaphoreType.DMA((3,))],
        compiler_params=pltpu.CompilerParams(vmem_limit_bytes=1024 * 1024),
    )(*out)
    return out[0], out[1].reshape(CB, 2, 8, NX), out[2]


def solution(mesh):
    ns = mesh.shape["slab"]
    specs = (P("chan", "slab", None, None), P(None, "chan", None), P("chan", "slab", None, None))
    out_specs = (
        P("chan", "slab", None, None),
        P("chan", "slab", None, None),
        P(None, "chan", None),
    )
    call = functools.partial(device_call, (2, 4, 2, ns // 2))
    return jax.shard_map(call, mesh=mesh, in_specs=specs, out_specs=out_specs, check_vma=False)
```
